256 devices in a mesh: dp: 4 (over x), ctx: 16 (over y_lo, z), tensor: 4 (over y_hi, core).
Axes of the slice: x: 4, y: 4 (y_hi: 2, y_lo: 2; y = y_hi * 2 + y_lo), z: 8, core: 2. Of those that a mesh axis runs over, the one named last changes fastest.
Arguments:
- layer_in: bfloat16 [4, 4096, 2048], P('dp', 'ctx'), may hold values from -6 to 6
- head_in: bfloat16 [4, 4096, 4096], P('dp', 'ctx', 'tensor'), may hold values from -6 to 6
- step_raw: float32 [4, 4096, 64], P('dp', 'ctx', 'tensor'), may hold values from -4 to 4
- step_bias: float32 [64], P('tensor'), may hold values from -4 to 0
- rate_log: float32 [64], P('tensor'), may hold values from -6 to 0
- skip_gain: float32 [64], P('tensor'), may hold values from 0.2 to 2
- inject_weight: bfloat16 [2048, 8, 256], P('dp', 'tensor'), may hold values from -0.03125 to 0.03125
- out_weight: bfloat16 [2048, 4096], P('dp', 'tensor'), may hold values from -0.125 to 0.125
- upstream: bfloat16 [4, 4096, 2048], P('dp', 'ctx'), may hold values from -6 to 6
- window_start: int32 [4], P('dp'), may hold values from 0 to 1023
- lengths: int32 [4], P('dp'), may hold values from 2048 to 4096
Outputs:
- layer_grad: bfloat16 [4, 4096, 2048], P('dp', 'ctx')
- head_grad: bfloat16 [4, 4096, 4096], P('dp', 'ctx', 'tensor')
- step_grad: float32 [4, 4096, 64], P('dp', 'ctx', 'tensor')
- out_weight_grad: float32 [2048, 4096], P(('dp', 'ctx'), 'tensor')
- inject_weight_grad: float32 [2048, 8, 256], P(('dp', 'ctx'), 'tensor')
The draws below stay inside these ranges and needn't reach their ends.
All inputs are finite; a program needn't handle non-finite values.
Results may differ from the reference program's by a relative error of at most 0.015.
Values may be sent and summed in bfloat16 or wider, within the bound.
A program may use at most 128 MiB of HBM per device.

```python
import jax
import jax.numpy as jnp
from jax import lax

D = 2048
DW = 2048
H = 64
P_SIZE = 64
N = 128
G = 8
BLOCK = 128
WINDOW = 4096
N_DP = 4


def plant(array, own_key, smallest, high):
    index_at = [jax.random.randint(jax.random.fold_in(own_key, axis), (), 0, length) for axis, length in enumerate(array.shape)]
    main_axis = array.shape.index(max(array.shape))
    neighbour = index_at[:main_axis] + [(index_at[main_axis] + 1) % array.shape[main_axis]] + index_at[main_axis + 1:]
    return array.at[tuple(index_at)].set(smallest).at[tuple(neighbour)].set(high)


def with_spikes(array, key, source, target, shards_of, factor):
    owner, partner = [(jnp.arange(array.shape[position]) // (array.shape[position] // shards_of)).reshape([-1 if axis == position else 1 for axis in range(array.ndim)]) for position in (source, target)]
    chosen = jax.random.permutation(key, shards_of)[partner]
    strong = (owner == chosen) | (owner == (partner + shards_of // 2) % shards_of)
    return jnp.where(strong, factor * array, array)


def block_scale(own_key, shape, pieces, smallest, top_value):
    def one(dim, parts):
        heights = jax.random.uniform(jax.random.fold_in(jax.random.fold_in(own_key, 6), dim), (parts,), jnp.float32, smallest / len(pieces), top_value / len(pieces))
        return jnp.repeat(jnp.exp(heights), shape[dim] // parts).reshape((-1,) + (1,) * (len(shape) - dim - 1))

    level = one(*pieces[0])
    for cut in pieces[1:]:
        level = level * one(*cut)
    return level


def bell_draw(stream_key, dims, width, most, pieces=(), kind=jnp.bfloat16):
    level = block_scale(stream_key, dims, pieces, -0.22, 0.18) if pieces else 1.0
    values = jax.random.normal(stream_key, dims, jnp.float32) * width * level
    return jnp.minimum(jnp.maximum(values, -most), most).astype(kind)


def heavy_noise(rng, extent, scale, limit, cuts, heavy, held_as=jnp.bfloat16):
    drawn = scale * jax.random.normal(rng, extent, jnp.float32)
    if cuts:
        drawn = drawn * block_scale(rng, extent, cuts, -0.22, 0.18)
    return jnp.clip(with_spikes(drawn, jax.random.fold_in(rng, 3), *heavy), -limit, limit).astype(held_as)


def setup_inputs(seed: int = 0) -> dict:
    seeds = jax.random.split(jax.random.key(seed), 12)
    layer_in = heavy_noise(seeds[0], (N_DP, WINDOW, D), 1.0, 6.0, ((0, 4), (1, 16)), (1, 2, 16, 2.0))
    head_in = bell_draw(seeds[1], (N_DP, WINDOW, H * P_SIZE), 1.0, 6.0, ((0, 4), (1, 16), (2, 4)))
    step_raw = bell_draw(seeds[2], (N_DP, WINDOW, H), 1.0, 4.0, ((0, 4), (1, 16), (2, 4)), jnp.float32)
    step_bias = jnp.clip(-4.0 + 4.0 * jax.random.uniform(seeds[3], (H,), jnp.float32) ** block_scale(seeds[3], (H,), ((0, 4),), -0.2, 0.2), -4.0, 0.0)
    rate_log = jnp.clip(-6.0 + 6.0 * jax.random.uniform(seeds[4], (H,), jnp.float32) ** block_scale(seeds[4], (H,), ((0, 4),), -0.2, 0.2), -6.0, 0.0)
    skip_gain = jnp.clip(0.2 + 1.8 * jax.random.uniform(seeds[5], (H,), jnp.float32) ** block_scale(seeds[5], (H,), ((0, 4),), -0.2, 0.2), 0.2, 2.0)
    inject_weight = bell_draw(seeds[6], (D, G, 2 * N), (D * 16) ** -0.5, 0.03125, ((0, 4), (1, 4)))
    out_weight = bell_draw(seeds[7], (DW, H * P_SIZE), DW ** -0.5, 0.125, ((0, 4), (1, 4)))
    upstream = heavy_noise(seeds[8], (N_DP, WINDOW, DW), 1.0, 6.0, ((0, 4), (1, 16)), (1, 2, 16, 2.0))
    window_start = plant(jax.random.randint(seeds[9], (N_DP,), 0, WINDOW // 4), jax.random.fold_in(seeds[9], 1), 0, (WINDOW // 4) - 1).astype(jnp.int32)
    lengths = plant(jax.random.randint(seeds[10], (N_DP,), WINDOW // 2, WINDOW + 1), jax.random.fold_in(seeds[10], 1), WINDOW // 2, WINDOW).astype(jnp.int32)
    return dict(layer_in=layer_in, head_in=head_in, step_raw=step_raw, step_bias=step_bias, rate_log=rate_log, skip_gain=skip_gain, inject_weight=inject_weight, out_weight=out_weight, upstream=upstream, window_start=window_start, lengths=lengths)


highest = lax.Precision.HIGHEST

def block_parts(head_values, inject, readout, steps, rates):
    log_decay = -steps * rates
    running = jnp.cumsum(log_decay, axis=1)
    scores = jnp.einsum('ctgn,csgn->ctsg', readout, inject, precision=highest)
    spread = running[:, :, None] - running[:, None, :]
    length = running.shape[1]
    causal = (jnp.arange(length)[:, None] >= jnp.arange(length)[None, :])[None, :, :, None, None]
    decays = jnp.exp(jnp.where(causal, spread, -jnp.inf))
    weighted = scores[..., None] * decays * steps[:, None]
    within = jnp.einsum('ctsgj,csgjp->ctgjp', weighted, head_values, precision=highest)
    tail_weight = jnp.exp(running[:, -1:] - running) * steps
    states = jnp.einsum('csgj,csgjp,csgn->cgjpn', tail_weight, head_values, inject, precision=highest)
    return (within, states, running[:, -1], running)

def block_outputs(within, states, totals, running, readout, head_values, skip_gain, state_in):

    def advance(carried, pair):
        return (jnp.exp(pair[1])[..., None, None] * carried + pair[0], carried)
    state_out, entering = lax.scan(advance, state_in, (states, totals))
    across = jnp.einsum('ctgn,cgjpn->ctgjp', readout, entering, precision=highest) * jnp.exp(running)[..., None]
    return (within + across + skip_gain[None, None, :, :, None] * head_values, state_out)

def layer_piece(values, coded, raw, state_in, masks, step_bias, rates, skip_gain, block_len):
    tokens = values.shape[0]
    groups = coded.shape[1]
    state_width = coded.shape[2] // 2
    heads = raw.shape[1]
    per_group = heads // groups
    head_width = values.shape[1] // heads
    block_count = tokens // block_len
    steps = masks[:, None] * jax.nn.softplus(raw + step_bias)
    head_values = values.reshape(block_count, block_len, groups, per_group, head_width)
    inject = coded[:, :, :state_width].reshape(block_count, block_len, groups, state_width)
    readout = coded[:, :, state_width:].reshape(block_count, block_len, groups, state_width)
    steps_four = steps.reshape(block_count, block_len, groups, per_group)
    within, states, totals, running = block_parts(head_values, inject, readout, steps_four, rates.reshape(groups, per_group))
    result, state_out = block_outputs(within, states, totals, running, readout, head_values, skip_gain.reshape(groups, per_group), state_in)
    result = result * masks.reshape(block_count, block_len)[:, :, None, None, None]
    return (result.reshape(tokens, heads * head_width), state_out)

def reference(layer_in, head_in, step_raw, step_bias, rate_log, skip_gain, inject_weight, out_weight, upstream, window_start, lengths):
    rates = jnp.exp(rate_log)
    flat_weight = inject_weight.reshape(D, G * 2 * N)
    positions = jnp.arange(WINDOW).astype(jnp.int32)
    contract_rows = (((0,), (0,)), ((), ()))
    contract_cols = (((1,), (1,)), ((), ()))

    def per_sequence(carried, sequence):
        weight_grad, inject_grad = carried
        masks = ((positions >= window_start[sequence]) & (positions < lengths[sequence])).astype(jnp.float32)
        projected = jnp.dot(layer_in[sequence], flat_weight, preferred_element_type=jnp.float32).astype(jnp.bfloat16)
        back_grad = jnp.dot(upstream[sequence], out_weight, preferred_element_type=jnp.float32).astype(jnp.bfloat16)
        zero_state = jnp.zeros((G, H // G, P_SIZE, N), jnp.float32)

        def forward(values, coded, raw):
            return layer_piece(values, coded, raw, zero_state, masks, step_bias, rates, skip_gain, BLOCK)[0]
        result, pullback = jax.vjp(forward, head_in[sequence].astype(jnp.float32), projected.reshape(WINDOW, G, 2 * N).astype(jnp.float32), step_raw[sequence])
        head_grad, coded_grad, raw_grad = pullback(back_grad.astype(jnp.float32))
        rounded = coded_grad.reshape(WINDOW, G * 2 * N).astype(jnp.bfloat16)
        layer_grad = lax.dot_general(rounded, flat_weight, contract_cols, preferred_element_type=jnp.float32).astype(jnp.bfloat16)
        weight_grad = weight_grad + lax.dot_general(upstream[sequence], result.astype(jnp.bfloat16), contract_rows, preferred_element_type=jnp.float32)
        inject_grad = inject_grad + lax.dot_general(layer_in[sequence], rounded, contract_rows, preferred_element_type=jnp.float32)
        return ((weight_grad, inject_grad), (layer_grad, head_grad.astype(jnp.bfloat16), raw_grad))
    initial = (jnp.zeros((DW, H * P_SIZE), jnp.float32), jnp.zeros((D, G * 2 * N), jnp.float32))
    (weight_grad, inject_grad), (layer_grad, head_grad, raw_grad) = lax.scan(per_sequence, initial, jnp.arange(N_DP).astype(jnp.int32))
    return (layer_grad, head_grad, raw_grad, weight_grad, inject_grad.reshape(D, G, 2 * N))
```

```python
import jax
import jax.numpy as jnp
from jax import lax
from jax.experimental import pallas as pl
from jax.experimental.pallas import tpu as pltpu
from jax.sharding import PartitionSpec as P

f32 = jnp.float32
bf16 = jnp.bfloat16
MESH = pl.DeviceIdType.MESH
ANY = pl.BlockSpec(memory_space=pl.ANY)
VM = pl.BlockSpec(memory_space=pltpu.VMEM)
LIMIT = 56 * 1024 * 1024
ROWS = (((0,), (0,)), ((), ()))
COLS = (((1,), (1,)), ((), ()))


def remote(src, dst, send, recv, where):
    return pltpu.make_async_remote_copy(
        src_ref=src, dst_ref=dst, send_sem=send, recv_sem=recv, device_id=where, device_id_type=MESH
    )


def greet(partners):
    barrier = pltpu.get_barrier_semaphore()
    for where in partners:
        pl.semaphore_signal(barrier, inc=1, device_id=where, device_id_type=MESH)
    pl.semaphore_wait(barrier, len(partners))


def places():
    x = lax.axis_index("dp")
    c = lax.axis_index("ctx")
    t = lax.axis_index("tensor")
    z = lax.rem(c, 8)
    base = c - z
    spots = dict(
        right={"dp": lax.rem(x + 1, 4)},
        left={"dp": lax.rem(x + 3, 4)},
        up={"ctx": base + lax.rem(z + 1, 8)},
        down={"ctx": base + lax.rem(z + 7, 8)},
        across={"ctx": lax.rem(c + 8, 16)},
        core={"tensor": t + 1 - 2 * lax.rem(t, 2)},
        far={"tensor": lax.rem(t + 2, 4)},
    )
    return x, c, t, z, spots


def dot(a, b, dims=None):
    if dims is None:
        return jnp.dot(a, b, preferred_element_type=f32)
    return lax.dot_general(a, b, dims, preferred_element_type=f32)


def pieces(v, count):
    found = []
    for _ in range(count):
        part = v.astype(bf16)
        found.append(part)
        v = v - part.astype(f32)
    return found


def split_left(v, m, count, dims=None):
    return sum(dot(part, m, dims) for part in pieces(v, count))


def split_right(m, v, count, dims=None):
    return sum(dot(m, part, dims) for part in pieces(v, count))


def weights_kernel(
    wi, wo, lin, up, proj, back, winj_out, wi_v, wo_v, lin_v, up_v, send, recv, local
):
    x, c, t, z, at = places()
    h = lax.rem(z, 2)
    lefts, rights, opposite = lax.rem(x + 3, 4), lax.rem(x + 1, 4), lax.rem(x + 2, 4)
    own = [(wi, wi_v), (wo, wo_v)]

    def rows(slab, half, q):
        return pl.ds(pl.multiple_of(slab * 512 + half * 256 + q * 128, 128), 128)

    loads = [
        pltpu.make_async_copy(wi, wi_v.at[pl.ds(pl.multiple_of(x * 512, 512), 512)], local.at[0]),
        pltpu.make_async_copy(wo, wo_v.at[pl.ds(pl.multiple_of(x * 512, 512), 512)], local.at[1]),
        pltpu.make_async_copy(lin, lin_v, local.at[2]),
        pltpu.make_async_copy(up, up_v, local.at[3]),
    ]
    for load in loads:
        load.start()
    greet([at["right"], at["left"], at["up"], at["down"]])

    sent = []

    def first(k, q, event, where):
        src, dst = own[k]
        s = remote(
            src.at[pl.ds(pl.multiple_of(h * 256 + q * 128, 128), 128)],
            dst.at[rows(x, h, q)],
            send.at[k, event],
            recv.at[k, event],
            where,
        )
        s.start()
        sent.append(s)

    def arrived(k, slab, half, q, event):
        dst = own[k][1].at[rows(slab, half, q)]
        remote(dst, dst, send.at[k, event], recv.at[k, event], at["left"]).wait_recv()

    def forward(k, slab, q, event, where):
        dst = own[k][1].at[rows(slab, h, q)]
        s = remote(dst, dst, send.at[k, event], recv.at[k, event], where)
        s.start()
        sent.append(s)

    for k in range(2):
        first(k, 0, 0, at["right"])
        first(k, 1, 2, at["left"])
        first(k, 1, 1, at["right"])
        first(k, 0, 3, at["left"])
    for k in range(2):
        arrived(k, lefts, h, 0, 0)
        forward(k, lefts, 0, 4, at["right"])
        forward(k, lefts, 0, 6, at["up"])
        arrived(k, rights, h, 1, 2)
        forward(k, rights, 1, 5, at["left"])
        forward(k, rights, 1, 10, at["down"])
        arrived(k, lefts, h, 1, 1)
        forward(k, lefts, 1, 9, at["down"])
        arrived(k, rights, h, 0, 3)
        forward(k, rights, 0, 7, at["up"])
    for k in range(2):
        arrived(k, opposite, h, 0, 4)
        forward(k, opposite, 0, 8, at["up"])
        arrived(k, opposite, h, 1, 5)
        forward(k, opposite, 1, 11, at["down"])
    for load in loads:
        load.wait()
    results = [(lin_v, proj), (up_v, back)]
    for k in range(2):
        for n, slab in enumerate((lefts, rights, opposite)):
            arrived(k, slab, 1 - h, 0, 6 + n)
            arrived(k, slab, 1 - h, 1, 9 + n)
        a, out = results[k]
        out[...] = dot(a[...], own[k][1][...]).astype(bf16)
        if k == 0:
            keep = pltpu.make_async_copy(wi_v, winj_out, local.at[0])
            keep.start()
    keep.wait()
    for s in sent:
        s.wait_send()


def weights_call(wi, wo, lin, up):
    return pl.pallas_call(
        weights_kernel,
        out_shape=(
            jax.ShapeDtypeStruct((256, 512), bf16),
            jax.ShapeDtypeStruct((256, 1024), bf16),
            jax.ShapeDtypeStruct((2048, 512), bf16),
        ),
        in_specs=[ANY] * 4,
        out_specs=(VM, VM, ANY),
        scratch_shapes=[
            pltpu.VMEM((2048, 512), bf16),
            pltpu.VMEM((2048, 1024), bf16),
            pltpu.VMEM((256, 2048), bf16),
            pltpu.VMEM((256, 2048), bf16),
            pltpu.SemaphoreType.DMA((2, 12)),
            pltpu.SemaphoreType.DMA((2, 12)),
            pltpu.SemaphoreType.DMA((4,)),
        ],
        compiler_params=pltpu.CompilerParams(
            collective_id=1, has_side_effects=True, vmem_limit_bytes=LIMIT
        ),
        name="weights",
    )(wi, wo, lin, up)


def iota(shape, axis):
    return lax.broadcasted_iota(jnp.int32, shape, axis)


def scan_kernel(
    x_ref, dt_ref, sig_ref, mask_ref, par_ref, proj_ref, back_ref, lin, up,
    res_ref, rnd_ref, hg_ref, sg_ref, linq, upq,
    y_s, z_s, xs_s, dy_s, ds_s, r_s, rt_s, msg, got, out, fin,
    send1, recv1, send2, recv2, send3, recv3, local,
):
    x, c, t, z, at = places()
    peers = [{"ctx": lax.rem(c + k, 16)} for k in range(1, 16)]
    greet(peers + [{"dp": lax.rem(x + k, 4)} for k in range(1, 4)])

    def quarter(j):
        return pl.ds(pl.multiple_of(j * 512, 512), 512)

    acts = []
    for n, (src, dst) in enumerate(((up, upq), (lin, linq))):
        for k in (1, 3, 2):
            to = lax.rem(x + k, 4)
            acts.append(
                remote(
                    src.at[:, quarter(to)], dst.at[x], send3.at[n, k], recv3.at[n, k], {"dp": to}
                )
            )
    own_up = pltpu.make_async_copy(up.at[:, quarter(x)], upq.at[x], local.at[0])
    own_lin = pltpu.make_async_copy(lin.at[:, quarter(x)], linq.at[x], local.at[1])
    own_up.start()
    own_lin.start()

    expand = jnp.where(
        (iota((128, 1024), 1) >= iota((128, 1024), 0) * 64)
        & (iota((128, 1024), 1) < iota((128, 1024), 0) * 64 + 64),
        1.0,
        0.0,
    ).astype(bf16)
    above = iota((256, 256), 0) >= iota((256, 256), 1)
    tril = jnp.where(above, 1.0, 0.0).astype(bf16)
    rate = par_ref[0:1, :]
    dt = dt_ref[...]
    running = split_right(tril, -dt * rate, 3)
    r_s[...] = running
    rt = jnp.transpose(running)
    rt_s[...] = rt[0:16, :]
    last = running[255:256, :]
    erx = split_left(jnp.exp(running), expand, 2)
    etx = split_left(jnp.exp(last - running), expand, 2)
    dtx = split_left(dt, expand, 2)
    xv = x_ref[...]
    mask = mask_ref[...]
    dy = (back_ref[...].astype(f32) * mask[:, 0:1]).astype(bf16)
    dy_s[...] = dy
    xs = (xv.astype(f32) * dtx).astype(bf16)
    xs_s[...] = xs
    xe = (xs.astype(f32) * etx).astype(bf16)
    de = (dy.astype(f32) * erx).astype(bf16)

    proj = proj_ref[...]
    inj = [proj[:, 256 * g : 256 * g + 128] for g in range(2)]
    rdo = [proj[:, 256 * g + 128 : 256 * g + 256] for g in range(2)]
    for g in range(2):
        span = slice(512 * g, 512 * g + 512)
        own = dot(xe[:, span], inj[g], ROWS)
        pull = dot(de[:, span], rdo[g], ROWS)
        msg[8 * g : 8 * g + 8, 0:64, :] = own.reshape(8, 64, 128).astype(bf16)
        msg[8 * g : 8 * g + 8, 64:128, :] = pull.reshape(8, 64, 128).astype(bf16)
    decay = jnp.broadcast_to(rt[0:16, 255:256], (16, 128))
    parts = pieces(decay, 3)
    row = iota((16, 16, 128), 1)
    lines = jnp.zeros((16, 16, 128), f32)
    for n, part in enumerate(parts):
        lines = jnp.where(row == n, part.astype(f32)[:, None, :], lines)
    msg[:, 128:144, :] = lines.astype(bf16)

    def to_peer(k):
        to = lax.rem(c + k, 16)
        return remote(msg.at[to], got.at[c], send1.at[k], recv1.at[k], {"ctx": to})

    def from_peer(k):
        who = lax.rem(c + 16 - k, 16)
        return remote(msg.at[who], got.at[who], send1.at[k], recv1.at[k], {"ctx": who})

    def to_peer2(k):
        to = lax.rem(c + k, 16)
        return remote(out.at[to], fin.at[c], send2.at[k], recv2.at[k], {"ctx": to})

    def from_peer2(k):
        who = lax.rem(c + 16 - k, 16)
        return remote(out.at[who], fin.at[who], send2.at[k], recv2.at[k], {"ctx": who})

    def each(fn):
        def body(k, carry):
            fn(k)
            return carry

        lax.fori_loop(1, 16, body, 0)

    each(lambda k: to_peer(k).start())
    for act in acts:
        act.start()
    got[c] = msg[c]

    side = iota((256, 128), 1)

    def group(g):
        bg, cg = inj[g], rdo[g]
        scores = dot(cg, bg, COLS)
        ds_s[g] = jnp.zeros((256, 256), f32)

        def pair(p, carry):
            at_lane = pl.ds(pl.multiple_of(512 * g + p * 128, 128), 128)
            x2 = xs_s[:, at_lane]
            dy2 = dy_s[:, at_lane]
            y2 = jnp.zeros((256, 128), f32)
            z2 = jnp.zeros((256, 128), f32)
            ds = ds_s[g]
            for half in range(2):
                head = 8 * g + 2 * p + half
                col = jnp.sum(jnp.where(side == head, r_s[...], 0.0), axis=1, keepdims=True)
                line = rt_s[pl.ds(head, 1), :]
                grow = jnp.exp(jnp.where(above, col - line, -1e30))
                mine = (side >= 64) if half else (side < 64)
                xm = jnp.where(mine, x2, jnp.zeros_like(x2))
                dm = jnp.where(mine, dy2, jnp.zeros_like(dy2))
                w = (scores * grow).astype(bf16)
                y2 += dot(w, xm)
                z2 += dot(w, dm, ROWS)
                ds += dot(dm, xm, COLS) * grow
            y_s[:, at_lane] = y2
            z_s[:, at_lane] = z2
            ds_s[g] = ds
            return carry

        lax.fori_loop(0, 4, pair, 0)

    group(0)

    each(lambda k: from_peer(k).wait_recv())

    def grow_of(k):
        lines = got[k, 128:144, :].astype(f32)
        return jnp.exp(lines[0:1] + lines[1:2] + lines[2:3])

    def ahead(k, state):
        out[k, 0:64, :] = state.astype(bf16)
        return grow_of(k) * state + got[k, 0:64, :].astype(f32)

    lax.fori_loop(0, 16, ahead, jnp.zeros((64, 128), f32))

    def behind(n, state):
        k = 15 - n
        out[k, 64:128, :] = state.astype(bf16)
        return grow_of(k) * state + got[k, 64:128, :].astype(f32)

    lax.fori_loop(0, 16, behind, jnp.zeros((64, 128), f32))
    each(lambda k: to_peer2(k).start())
    fin[c] = out[c]

    group(1)

    each(lambda k: from_peer2(k).wait_recv())

    skipx = split_left(jnp.broadcast_to(par_ref[1:2, :], (8, 128)), expand, 3)[0:1, :]
    sums_q = jnp.zeros((256, 128), f32)
    sums_v = jnp.zeros((256, 128), f32)
    sums_u = jnp.zeros((256, 128), f32)
    ends = jnp.zeros((8, 128), f32)
    ones = jnp.ones((8, 128), bf16)
    for g in range(2):
        span = slice(512 * g, 512 * g + 512)
        bg, cg = inj[g], rdo[g]
        state = fin[8 * g : 8 * g + 8, 0:64, :].reshape(512, 128)
        later = fin[8 * g : 8 * g + 8, 64:128, :].reshape(512, 128)
        ex = expand[:, span]
        ya = dot(cg, state, COLS) * erx[:, span]
        zs = dot(bg, later, COLS) * etx[:, span]
        dsr = ds_s[g].astype(bf16)
        db = dot(dsr, cg, ROWS) + dot(xe[:, span], later)
        dc = dot(dsr, bg) + dot(de[:, span], state)
        rnd_ref[:, 256 * g : 256 * g + 128] = db.astype(bf16)
        rnd_ref[:, 256 * g + 128 : 256 * g + 256] = dc.astype(bf16)
        xg = xv[:, span].astype(f32)
        xsg = xs[:, span].astype(f32)
        dyg = dy[:, span].astype(f32)
        zw = z_s[:, span]
        yt = y_s[:, span] + ya
        zt = zw + zs
        res_ref[:, span] = (mask[:, 0:1] * (yt + skipx[:, span] * xg)).astype(bf16)
        hg_ref[:, span] = (dtx[:, span] * zt + skipx[:, span] * dyg).astype(bf16)
        sums_q += split_left(dyg * yt - xsg * zw, ex, 3, COLS)
        sums_v += split_left(xsg * zs, ex, 2, COLS)
        sums_u += split_left(xg * zt, ex, 2, COLS)
        rows = split_right(ones, state.astype(f32) * later.astype(f32), 2, COLS)
        ends += split_left(rows, ex, 2, COLS)
    triu = jnp.where(iota((256, 256), 0) <= iota((256, 256), 1), 1.0, 0.0).astype(bf16)
    lower = jnp.where(iota((256, 256), 0) > iota((256, 256), 1), 1.0, 0.0).astype(bf16)
    flow = split_right(triu, sums_q, 3) + split_right(lower, sums_v, 3)
    flow = flow + ends[0:1, :] * jnp.exp(last)
    sg_ref[...] = sig_ref[...] * (sums_u - rate * flow)

    own_up.wait()
    own_lin.wait()
    for n, (src, dst) in enumerate(((up, upq), (lin, linq))):
        for k in (1, 3, 2):
            who = lax.rem(x + 4 - k, 4)
            remote(
                src.at[:, quarter(who)], dst.at[who], send3.at[n, k], recv3.at[n, k], {"dp": who}
            ).wait_recv()
    for act in acts:
        act.wait_send()
    each(lambda k: to_peer(k).wait_send())
    each(lambda k: to_peer2(k).wait_send())


def scan_call(x, dt, sig, mask, par, proj, back, lin, up):
    quarters = jax.ShapeDtypeStruct((4, 256, 512), bf16)
    return pl.pallas_call(
        scan_kernel,
        out_shape=(
            jax.ShapeDtypeStruct((256, 1024), bf16),
            jax.ShapeDtypeStruct((256, 512), bf16),
            jax.ShapeDtypeStruct((256, 1024), bf16),
            jax.ShapeDtypeStruct((256, 128), f32),
            quarters,
            quarters,
        ),
        in_specs=[VM] * 7 + [ANY] * 2,
        out_specs=(VM, VM, VM, VM, ANY, ANY),
        scratch_shapes=[
            pltpu.VMEM((256, 1024), f32),
            pltpu.VMEM((256, 1024), f32),
            pltpu.VMEM((256, 1024), bf16),
            pltpu.VMEM((256, 1024), bf16),
            pltpu.VMEM((2, 256, 256), f32),
            pltpu.VMEM((256, 128), f32),
            pltpu.VMEM((16, 256), f32),
            pltpu.VMEM((16, 144, 128), bf16),
            pltpu.VMEM((16, 144, 128), bf16),
            pltpu.VMEM((16, 128, 128), bf16),
            pltpu.VMEM((16, 128, 128), bf16),
            pltpu.SemaphoreType.DMA((16,)),
            pltpu.SemaphoreType.DMA((16,)),
            pltpu.SemaphoreType.DMA((16,)),
            pltpu.SemaphoreType.DMA((16,)),
            pltpu.SemaphoreType.DMA((2, 4)),
            pltpu.SemaphoreType.DMA((2, 4)),
            pltpu.SemaphoreType.DMA((2,)),
        ],
        compiler_params=pltpu.CompilerParams(
            collective_id=2, has_side_effects=True, vmem_limit_bytes=LIMIT
        ),
        name="scan",
    )(x, dt, sig, mask, par, proj, back, lin, up)


def grads_kernel(
    res, rnd, linq, upq, winj, lg, wg, ig,
    factor, act, w_v, rnd_v, part, half_in, pair_out, pair_in, acc, ring_out, ring_in, y_out, y_in,
    send, recv, zsend, zrecv, ysend, yrecv, tsend, trecv, local,
):
    x, c, t, z, at = places()
    yl = lax.div(c, 8)
    cr = lax.rem(t, 2)
    lefts, rights, opposite = lax.rem(x + 3, 4), lax.rem(x + 1, 4), lax.rem(x + 2, 4)
    source = [res.at[:, 0:512], res.at[:, 512:1024], rnd]
    loads = [
        pltpu.make_async_copy(source[g], factor.at[g, x], local.at[g]) for g in range(3)
    ] + [
        pltpu.make_async_copy(upq, act.at[0], local.at[3]),
        pltpu.make_async_copy(linq, act.at[1], local.at[4]),
        pltpu.make_async_copy(winj, w_v, local.at[5]),
        pltpu.make_async_copy(rnd, rnd_v, local.at[6]),
    ]
    for load in loads:
        load.start()
    greet([at[k] for k in ("right", "left", "up", "down", "across", "core", "far")])
    sent = []

    def go(copy):
        copy.start()
        sent.append(copy)

    def rows(q):
        return pl.ds(q * 128, 128)

    def first(g, q, event, where):
        go(
            remote(
                source[g].at[rows(q)],
                factor.at[g, x, rows(q)],
                send.at[g, event],
                recv.at[g, event],
                where,
            )
        )

    def arrived(g, slab, q, event):
        dst = factor.at[g, slab, rows(q)]
        remote(dst, dst, send.at[g, event], recv.at[g, event], at["left"]).wait_recv()

    def forward(g, slab, q, event, where):
        dst = factor.at[g, slab, rows(q)]
        go(remote(dst, dst, send.at[g, event], recv.at[g, event], where))

    for g in range(3):
        first(g, 0, 0, at["right"])
        first(g, 1, 2, at["left"])
        first(g, 1, 1, at["right"])
        first(g, 0, 3, at["left"])

    def relay(g):
        arrived(g, lefts, 0, 0)
        forward(g, lefts, 0, 4, at["right"])
        arrived(g, rights, 1, 2)
        forward(g, rights, 1, 5, at["left"])

    def product(g):
        arrived(g, lefts, 1, 1)
        arrived(g, rights, 0, 3)
        arrived(g, opposite, 0, 4)
        arrived(g, opposite, 1, 5)
        a = act[0 if g < 2 else 1].reshape(1024, 512)
        acc[g] = dot(a, factor[g].reshape(1024, 512), ROWS).reshape(16, 32, 512)

    def piece(g, d, k):
        lanes = slice(256 * d, 256 * d + 256)
        return acc[g, k, :, lanes], acc[g, 8 + k, :, lanes]

    def ring(g, step):
        for d in range(2):
            k = lax.rem(z + 15 - step, 8) if d == 0 else lax.rem(z + 1 + step, 8)
            low, high = piece(g, d, k)
            if step > 0:
                came = ring_in.at[g, d, step - 1]
                remote(
                    came, came, zsend.at[g, d, step - 1], zrecv.at[g, d, step - 1], at["up"]
                ).wait_recv()
                low += came[0].astype(f32)
                high += came[1].astype(f32)
            if step < 7:
                ring_out[g, d, step, 0] = low.astype(bf16)
                ring_out[g, d, step, 1] = high.astype(bf16)
                go(
                    remote(
                        ring_out.at[g, d, step],
                        ring_in.at[g, d, step],
                        zsend.at[g, d, step],
                        zrecv.at[g, d, step],
                        at["up"] if d == 0 else at["down"],
                    )
                )
            else:
                lanes = slice(256 * d, 256 * d + 256)
                acc[g, z, :, lanes] = low
                acc[g, 8 + z, :, lanes] = high
        if step == 7:
            y_out[g] = acc[g, (1 - yl) * 8 + z].astype(bf16)
            go(
                remote(y_out.at[g], y_in.at[g], ysend.at[g], yrecv.at[g], at["across"])
            )

    def finish(g):
        remote(y_out.at[g], y_in.at[g], ysend.at[g], yrecv.at[g], at["across"]).wait_recv()
        total = acc[g, c] + y_in[g].astype(f32)
        if g < 2:
            wg[:, 512 * g : 512 * g + 512] = total
        else:
            ig[...] = total

    mine = pl.ds(pl.multiple_of(cr * 128, 128), 128)
    other = pl.ds(pl.multiple_of((1 - cr) * 128, 128), 128)
    loads[5].wait()
    loads[6].wait()
    part[...] = dot(rnd_v[...], w_v[...], COLS)
    half_in[1] = part[other, :].astype(bf16)
    go(remote(half_in.at[1], half_in.at[0], tsend.at[0], trecv.at[0], at["core"]))
    for load in loads[:5]:
        load.wait()
    relay(0)
    remote(half_in.at[1], half_in.at[0], tsend.at[0], trecv.at[0], at["core"]).wait_recv()
    pair_out[...] = (part[mine, :] + half_in[0].astype(f32)).astype(bf16)
    go(remote(pair_out, pair_in, tsend.at[1], trecv.at[1], at["far"]))
    relay(1)
    product(0)
    ring(0, 0)
    ring(0, 1)
    relay(2)
    ring(0, 2)
    product(1)
    ring(0, 3)
    ring(1, 0)
    ring(0, 4)
    ring(1, 1)
    ring(0, 5)
    ring(1, 2)
    product(2)
    ring(0, 6)
    ring(1, 3)
    ring(2, 0)
    remote(pair_out, pair_in, tsend.at[1], trecv.at[1], at["far"]).wait_recv()
    lg[mine, :] = (pair_out[...].astype(f32) + pair_in[...].astype(f32)).astype(bf16)
    go(remote(lg.at[mine], lg.at[mine], tsend.at[2], trecv.at[2], at["core"]))
    ring(0, 7)
    ring(1, 4)
    ring(2, 1)
    ring(1, 5)
    ring(2, 2)
    ring(1, 6)
    ring(2, 3)
    ring(1, 7)
    ring(2, 4)
    finish(0)
    ring(2, 5)
    ring(2, 6)
    finish(1)
    ring(2, 7)
    finish(2)
    remote(lg.at[other], lg.at[other], tsend.at[2], trecv.at[2], at["core"]).wait_recv()
    for s in sent:
        s.wait_send()


def grads_call(res, rnd, linq, upq, winj):
    return pl.pallas_call(
        grads_kernel,
        out_shape=(
            jax.ShapeDtypeStruct((256, 2048), bf16),
            jax.ShapeDtypeStruct((32, 1024), f32),
            jax.ShapeDtypeStruct((32, 512), f32),
        ),
        in_specs=[ANY] * 5,
        out_specs=(VM, VM, VM),
        scratch_shapes=[
            pltpu.VMEM((3, 4, 256, 512), bf16),
            pltpu.VMEM((2, 4, 256, 512), bf16),
            pltpu.VMEM((2048, 512), bf16),
            pltpu.VMEM((256, 512), bf16),
            pltpu.VMEM((256, 2048), f32),
            pltpu.VMEM((2, 128, 2048), bf16),
            pltpu.VMEM((128, 2048), bf16),
            pltpu.VMEM((128, 2048), bf16),
            pltpu.VMEM((3, 16, 32, 512), f32),
            pltpu.VMEM((3, 2, 7, 2, 32, 256), bf16),
            pltpu.VMEM((3, 2, 7, 2, 32, 256), bf16),
            pltpu.VMEM((3, 32, 512), bf16),
            pltpu.VMEM((3, 32, 512), bf16),
            pltpu.SemaphoreType.DMA((3, 6)),
            pltpu.SemaphoreType.DMA((3, 6)),
            pltpu.SemaphoreType.DMA((3, 2, 7)),
            pltpu.SemaphoreType.DMA((3, 2, 7)),
            pltpu.SemaphoreType.DMA((3,)),
            pltpu.SemaphoreType.DMA((3,)),
            pltpu.SemaphoreType.DMA((3,)),
            pltpu.SemaphoreType.DMA((3,)),
            pltpu.SemaphoreType.DMA((7,)),
        ],
        compiler_params=pltpu.CompilerParams(
            collective_id=3, has_side_effects=True, vmem_limit_bytes=LIMIT
        ),
        name="grads",
    )(res, rnd, linq, upq, winj)


def per_device(
    layer_in, head_in, step_raw, step_bias, rate_log, skip_gain,
    inject_weight, out_weight, upstream, window_start, lengths,
):
    tokens = head_in.shape[1]
    inputs, incoming = layer_in[0], upstream[0]
    wi = inject_weight.reshape(512, 512)
    positions = lax.axis_index("ctx") * tokens + jnp.arange(tokens, dtype=jnp.int32)
    mask = ((positions >= window_start[0]) & (positions < lengths[0])).astype(f32)[:, None]
    shifted = step_raw[0] + step_bias
    wide = ((0, 0), (0, 112))
    dt = jnp.pad(mask * jax.nn.softplus(shifted), wide)
    sig = jnp.pad(mask * jax.nn.sigmoid(shifted), wide)
    par = jnp.pad(jnp.stack([jnp.exp(rate_log), skip_gain]), ((0, 6), (0, 112)))
    masks = jnp.broadcast_to(mask, (tokens, 128))
    proj, back, winj = weights_call(wi, out_weight, inputs, incoming)
    res, rnd, hg, sg, linq, upq = scan_call(
        head_in[0], dt, sig, masks, par, proj, back, inputs, incoming
    )
    lg, wg, ig = grads_call(res, rnd, linq, upq, winj)
    return lg[None], hg[None], sg[None, :, :16], wg, ig.reshape(32, 2, 256)


def solution(mesh):
    placed = (
        P("dp", "ctx", None),
        P("dp", "ctx", "tensor"),
        P("dp", "ctx", "tensor"),
        P("tensor"),
        P("tensor"),
        P("tensor"),
        P("dp", "tensor", None),
        P("dp", "tensor"),
        P("dp", "ctx", None),
        P("dp"),
        P("dp"),
    )
    return jax.shard_map(
        per_device,
        mesh=mesh,
        in_specs=placed,
        out_specs=(
            P("dp", "ctx", None),
            P("dp", "ctx", "tensor"),
            P("dp", "ctx", "tensor"),
            P(("dp", "ctx"), "tensor"),
            P(("dp", "ctx"), "tensor", None),
        ),
        check_vma=False,
    )
```

```python
import jax
import jax.numpy as jnp
from jax import lax
from jax.experimental import pallas as pl
from jax.experimental.pallas import tpu as pltpu
from jax.sharding import PartitionSpec as P

f32 = jnp.float32
bf16 = jnp.bfloat16
MESH = pl.DeviceIdType.MESH
ANY = pl.BlockSpec(memory_space=pl.ANY)
VM = pl.BlockSpec(memory_space=pltpu.VMEM)
WINDOW = 2
LIMIT = 56 * 1024 * 1024
ROWS = (((0,), (0,)), ((), ()))
COLS = (((1,), (1,)), ((), ()))


def remote(src, dst, send, recv, where):
    return pltpu.make_async_remote_copy(
        src_ref=src, dst_ref=dst, send_sem=send, recv_sem=recv, device_id=where, device_id_type=MESH
    )


def greet(partners):
    barrier = pltpu.get_barrier_semaphore()
    for where in partners:
        pl.semaphore_signal(barrier, inc=1, device_id=where, device_id_type=MESH)
    pl.semaphore_wait(barrier, len(partners))


def places():
    x = lax.axis_index("dp")
    c = lax.axis_index("ctx")
    t = lax.axis_index("tensor")
    z = lax.rem(c, 8)
    base = c - z
    spots = dict(
        right={"dp": lax.rem(x + 1, 4)},
        left={"dp": lax.rem(x + 3, 4)},
        up={"ctx": base + lax.rem(z + 1, 8)},
        down={"ctx": base + lax.rem(z + 7, 8)},
        across={"ctx": lax.rem(c + 8, 16)},
        core={"tensor": t + 1 - 2 * lax.rem(t, 2)},
        far={"tensor": lax.rem(t + 2, 4)},
    )
    return x, c, t, z, spots


def dot(a, b, dims=None):
    if dims is None:
        return jnp.dot(a, b, preferred_element_type=f32)
    return lax.dot_general(a, b, dims, preferred_element_type=f32)


def pieces(v, count):
    found = []
    for _ in range(count):
        part = v.astype(bf16)
        found.append(part)
        v = v - part.astype(f32)
    return found


def split_left(v, m, count, dims=None):
    return sum(dot(part, m, dims) for part in pieces(v, count))


def split_right(m, v, count, dims=None):
    return sum(dot(m, part, dims) for part in pieces(v, count))


def iota(shape, axis):
    return lax.broadcasted_iota(jnp.int32, shape, axis)


class Lane:
    def __init__(self, window):
        self.window = window
        self.sent = []
        self.waited = 0

    def push(self, copy):
        while len(self.sent) - self.waited >= self.window:
            self.sent[self.waited].wait_send()
            self.waited += 1
        copy.start()
        self.sent.append(copy)

    def drain(self):
        while self.waited < len(self.sent):
            self.sent[self.waited].wait_send()
            self.waited += 1


def kernel(
    x_ref, raw_ref, bias_ref, rate_ref, skip_ref, start_ref, stop_ref, wi, wo, lin, up,
    lg, hg_ref, sg_ref, wg, ig,
    wi_v, wo_v, lin_v, up_v, proj_s, back_s, y_s, z_s, xs_s, xe_s, dy_s, de_s, erx_s, etx_s, dtx_s, ds_s,
    r_s, rt_s, f_out, f_got, f_mid, f_fin, b_out, b_got, b_mid, b_fin,
    factor, act, part, half_out, half_in, pair_out, pair_in, acc, ring_out, ring_in, y_out, y_in,
    wsend, wrecv, asend, arecv, csend, crecv, esend, erecv,
    send, recv, zsend, zrecv, ysend, yrecv, tsend, trecv, local,
):
    x, c, t, z, at = places()
    h = lax.rem(z, 2)
    yl = lax.div(c, 8)
    cr = lax.rem(t, 2)
    lefts, rights, opposite = lax.rem(x + 3, 4), lax.rem(x + 1, 4), lax.rem(x + 2, 4)
    mine = pl.ds(pl.multiple_of(cr * 128, 128), 128)
    other = pl.ds(pl.multiple_of((1 - cr) * 128, 128), 128)

    def quarter(j):
        return pl.ds(pl.multiple_of(j * 512, 512), 512)

    loads = [
        pltpu.make_async_copy(wi, wi_v.at[quarter(x)], local.at[0]),
        pltpu.make_async_copy(wo, wo_v.at[quarter(x)], local.at[1]),
        pltpu.make_async_copy(lin, lin_v, local.at[2]),
        pltpu.make_async_copy(up, up_v, local.at[3]),
    ]
    for load in loads:
        load.start()
    greet(
        [at[k] for k in ("right", "left", "core", "far")]
        + [{"dp": opposite}]
        + [{"ctx": lax.rem(c + k, 16)} for k in range(1, 16)]
    )

    links = {k: Lane(WINDOW) for k in ("right", "left", "up", "down")}

    def strip(ref, g):
        return ref if g == 0 else ref.at[:, 512 * (g - 1) : 512 * g]

    def weight_rows(g, slab, half, q):
        rows = pl.ds(pl.multiple_of(slab * 512 + half * 256 + q * 128, 128), 128)
        return strip(wi_v if g == 0 else wo_v, g).at[rows]

    def first(g, q, event, way):
        rows = pl.ds(pl.multiple_of(h * 256 + q * 128, 128), 128)
        links[way].push(
            remote(
                strip(wi if g == 0 else wo, g).at[rows],
                weight_rows(g, x, h, q),
                wsend.at[g, event],
                wrecv.at[g, event],
                at[way],
            )
        )

    def arrived(g, slab, half, q, event):
        dst = weight_rows(g, slab, half, q)
        remote(dst, dst, wsend.at[g, event], wrecv.at[g, event], at["left"]).wait_recv()

    def forward(g, slab, q, event, way):
        dst = weight_rows(g, slab, h, q)
        links[way].push(remote(dst, dst, wsend.at[g, event], wrecv.at[g, event], at[way]))

    def slot(g, n):
        if n == 0:
            first(g, 0, 0, "right")
            first(g, 1, 2, "left")
        elif n == 1:
            first(g, 1, 1, "right")
            first(g, 0, 3, "left")
        elif n == 2:
            arrived(g, lefts, h, 0, 0)
            forward(g, lefts, 0, 4, "right")
            arrived(g, rights, h, 1, 2)
            forward(g, rights, 1, 5, "left")
            forward(g, lefts, 0, 6, "up")
            forward(g, rights, 1, 10, "down")
        elif n == 3:
            arrived(g, lefts, h, 1, 1)
            forward(g, lefts, 1, 9, "down")
            arrived(g, rights, h, 0, 3)
            forward(g, rights, 0, 7, "up")
        else:
            arrived(g, opposite, h, 0, 4)
            forward(g, opposite, 0, 8, "up")
            arrived(g, opposite, h, 1, 5)
            forward(g, opposite, 1, 11, "down")

    def gathered(g):
        for n, slab in enumerate((lefts, rights, opposite)):
            arrived(g, slab, 1 - h, 0, 6 + n)
            arrived(g, slab, 1 - h, 1, 9 + n)

    def swap(e, src, dst):
        def to_peer(k):
            to = lax.rem(c + k, 16)
            return remote(src.at[to], dst.at[c], esend.at[e, k], erecv.at[e, k], {"ctx": to})

        def from_peer(k):
            who = lax.rem(c + 16 - k, 16)
            return remote(src.at[who], dst.at[who], esend.at[e, k], erecv.at[e, k], {"ctx": who})

        def each(fn):
            def step(k, carry):
                fn(k)
                return carry

            lax.fori_loop(1, 16, step, 0)

        def begin():
            each(lambda k: to_peer(k).start())
            dst[c] = src[c]

        return (
            begin,
            lambda: each(lambda k: from_peer(k).wait_recv()),
            lambda: each(lambda k: to_peer(k).wait_send()),
        )

    f1 = swap(0, f_out, f_got)
    f2 = swap(1, f_mid, f_fin)
    b1 = swap(2, b_out, b_got)
    b2 = swap(3, b_mid, b_fin)

    slot(0, 0)
    slot(0, 1)

    side16 = iota((16, 1024), 1) - 64 * iota((16, 1024), 0)
    expand = jnp.where((side16 >= 0) & (side16 < 64), 1.0, 0.0).astype(bf16)
    above = iota((256, 256), 0) >= iota((256, 256), 1)
    tril = jnp.where(above, 1.0, 0.0).astype(bf16)
    eye = jnp.where(iota((256, 256), 0) == iota((256, 256), 1), 1.0, 0.0).astype(bf16)
    position = c * 256 + iota((256, 1), 0)
    mask = jnp.where((position >= start_ref[...]) & (position < stop_ref[...]), 1.0, 0.0)
    rate = jnp.exp(rate_ref[...])
    shifted = raw_ref[...] + bias_ref[...]
    small = jnp.exp(-jnp.abs(shifted))
    dt = mask * (jnp.maximum(shifted, 0.0) + jnp.log1p(small))
    sig = mask * jnp.where(shifted >= 0.0, 1.0, small) / (1.0 + small)
    running = split_right(tril, -dt * rate, 3)
    r_s[...] = running
    rt = split_left(running, eye, 3, ROWS)
    rt_s[...] = rt
    last = running[255:256, :]
    erx_s[...] = split_left(jnp.exp(running), expand, 2)
    etx_s[...] = split_left(jnp.exp(last - running), expand, 2)
    dtx_s[...] = split_left(dt, expand, 2)
    xs_s[...] = (x_ref[...].astype(f32) * dtx_s[...]).astype(bf16)
    xe_s[...] = (xs_s[...].astype(f32) * etx_s[...]).astype(bf16)
    skipx = split_left(jnp.broadcast_to(skip_ref[...], (8, 16)), expand, 3)[0:1, :]
    decay = jnp.broadcast_to(rt[:, 255:256], (16, 128))
    row = iota((16, 16, 128), 1)
    lines = jnp.zeros((16, 16, 128), f32)
    for n, term in enumerate(pieces(decay, 3)):
        lines = jnp.where(row == n, term.astype(f32)[:, None, :], lines)
    f_out[:, 64:80, :] = lines.astype(bf16)

    slot(0, 2)
    slot(1, 0)
    slot(0, 3)
    slot(1, 1)
    slot(0, 4)
    for load in loads:
        load.wait()
    gathered(0)

    def spans(g):
        return slice(512 * g, 512 * g + 512)

    def bs(g):
        return proj_s[:, 256 * g : 256 * g + 128]

    def cs(g):
        return proj_s[:, 256 * g + 128 : 256 * g + 256]

    proj_s[...] = dot(lin_v[...], wi_v[...]).astype(bf16)
    for g in range(2):
        own = dot(xe_s[:, spans(g)], bs(g), ROWS)
        f_out[8 * g : 8 * g + 8, 0:64, :] = own.reshape(8, 64, 128).astype(bf16)
    f1[0]()
    slot(1, 2)
    slot(2, 0)
    slot(1, 3)
    slot(2, 1)
    slot(1, 4)
    slot(2, 2)

    def grow_of(k):
        lines = f_got[k, 64:80, :].astype(f32)
        return jnp.exp(lines[0:1] + lines[1:2] + lines[2:3])

    f1[1]()

    def ahead(k, state):
        f_mid[k] = state.astype(bf16)
        return grow_of(k) * state + f_got[k, 0:64, :].astype(f32)

    lax.fori_loop(0, 16, ahead, jnp.zeros((64, 128), f32))
    f2[0]()
    slot(2, 3)
    slot(2, 4)

    values = (up_v, lin_v)
    acts = []

    def act_send(n):
        for k in (1, 3, 2):
            to = lax.rem(x + k, 4)
            copy = remote(
                values[n].at[mine, quarter(to)],
                act.at[n, x, mine],
                asend.at[n, k],
                arecv.at[n, k],
                {"dp": to},
            )
            copy.start()
            acts.append(copy)
        act[n, x] = values[n][:, quarter(x)]

    def act_share(n):
        for k in (1, 3, 2):
            dst = act.at[n, lax.rem(x + 4 - k, 4), mine]
            remote(dst, dst, asend.at[n, k], arecv.at[n, k], at["left"]).wait_recv()
            copy = remote(dst, dst, csend.at[n, k], crecv.at[n, k], at["core"])
            copy.start()
            acts.append(copy)

    def act_done(n):
        for k in (1, 3, 2):
            dst = act.at[n, lax.rem(x + 4 - k, 4), other]
            remote(dst, dst, csend.at[n, k], crecv.at[n, k], at["core"]).wait_recv()

    act_send(0)
    gathered(1)
    gathered(2)
    act_send(1)
    back = dot(up_v[...], wo_v[...]).astype(bf16).astype(f32)
    dy_s[...] = (back * mask).astype(bf16)
    de_s[...] = (dy_s[...].astype(f32) * erx_s[...]).astype(bf16)
    for g in range(2):
        pull = dot(de_s[:, spans(g)], cs(g), ROWS)
        b_out[8 * g : 8 * g + 8] = pull.reshape(8, 64, 128).astype(bf16)
    b1[0]()

    side = iota((256, 128), 1)
    side16 = iota((256, 16), 1)

    def group(g):
        bg, cg = bs(g), cs(g)
        scores = dot(cg, bg, COLS)
        ds_s[g] = jnp.zeros((256, 256), f32)

        def pair(p, carry):
            lanes = pl.ds(pl.multiple_of(512 * g + p * 128, 128), 128)
            x2 = xs_s[:, lanes]
            dy2 = dy_s[:, lanes]
            y2 = jnp.zeros((256, 128), f32)
            z2 = jnp.zeros((256, 128), f32)
            ds = ds_s[g]
            for half in range(2):
                head = 8 * g + 2 * p + half
                col = jnp.sum(jnp.where(side16 == head, r_s[...], 0.0), axis=1, keepdims=True)
                line = rt_s[pl.ds(head, 1), :]
                grow = jnp.exp(jnp.where(above, col - line, -1e30))
                here = (side >= 64) if half else (side < 64)
                xm = jnp.where(here, x2, jnp.zeros_like(x2))
                dm = jnp.where(here, dy2, jnp.zeros_like(dy2))
                w = (scores * grow).astype(bf16)
                y2 += dot(w, xm)
                z2 += dot(w, dm, ROWS)
                ds += dot(dm, xm, COLS) * grow
            y_s[:, lanes] = y2
            z_s[:, lanes] = z2
            ds_s[g] = ds
            return carry

        lax.fori_loop(0, 4, pair, 0)

    group(0)
    group(1)

    def states(fin, g):
        return fin[8 * g : 8 * g + 8].reshape(512, 128)

    sent = []

    def go(copy):
        copy.start()
        sent.append(copy)

    def own_send(g):
        rows = [pl.ds(0, 128), pl.ds(128, 128)]
        for q, event, way in ((0, 0, "right"), (1, 2, "left"), (1, 1, "right"), (0, 3, "left")):
            src = factor.at[g, x, rows[q]]
            go(remote(src, src, send.at[g, event], recv.at[g, event], at[way]))

    def came(g, slab, q, event):
        dst = factor.at[g, slab, pl.ds(128 * q, 128)]
        remote(dst, dst, send.at[g, event], recv.at[g, event], at["left"]).wait_recv()
        return dst

    def relay(g):
        src = came(g, lefts, 0, 0)
        go(remote(src, src, send.at[g, 4], recv.at[g, 4], at["right"]))
        src = came(g, rights, 1, 2)
        go(remote(src, src, send.at[g, 5], recv.at[g, 5], at["left"]))

    f2[1]()
    for g in range(2):
        span = spans(g)
        ya = dot(cs(g), states(f_fin, g), COLS) * erx_s[:, span]
        yt = y_s[:, span] + ya
        y_s[:, span] = yt
        value = mask * (yt + skipx[:, span] * x_ref[:, span].astype(f32))
        factor[g, x] = value.astype(bf16)
        own_send(g)

    b1[1]()

    def behind(n, state):
        k = 15 - n
        b_mid[k] = state.astype(bf16)
        return grow_of(k) * state + b_got[k].astype(f32)

    lax.fori_loop(0, 16, behind, jnp.zeros((64, 128), f32))
    b2[0]()
    act_share(0)
    relay(0)
    relay(1)
    act_share(1)
    b2[1]()

    for g in range(2):
        later = states(b_fin, g)
        state = states(f_fin, g)
        dsr = ds_s[g].astype(bf16)
        db = dot(dsr, cs(g), ROWS) + dot(xe_s[:, spans(g)], later)
        dc = dot(dsr, bs(g)) + dot(de_s[:, spans(g)], state)
        factor[2, x, :, 256 * g : 256 * g + 128] = db.astype(bf16)
        factor[2, x, :, 256 * g + 128 : 256 * g + 256] = dc.astype(bf16)
    own_send(2)
    part[...] = dot(factor[2, x], wi_v[...], COLS)
    half_out[...] = part[other, :].astype(bf16)
    go(remote(half_out, half_in, tsend.at[0], trecv.at[0], at["core"]))

    def product(g):
        came(g, lefts, 1, 1)
        came(g, rights, 0, 3)
        came(g, opposite, 0, 4)
        came(g, opposite, 1, 5)
        a = act[0 if g < 2 else 1].reshape(1024, 512)
        acc[g] = dot(a, factor[g].reshape(1024, 512), ROWS).reshape(16, 32, 512)

    def pass_on(g, k, slot_in, slot_out, way):
        low, high = acc[g, k], acc[g, 8 + k]
        if slot_in is not None:
            got = ring_in.at[g, slot_in]
            remote(got, got, zsend.at[g, slot_in], zrecv.at[g, slot_in], at["up"]).wait_recv()
            low += got[0].astype(f32)
            high += got[1].astype(f32)
        ring_out[g, slot_out, 0] = low.astype(bf16)
        ring_out[g, slot_out, 1] = high.astype(bf16)
        go(
            remote(
                ring_out.at[g, slot_out],
                ring_in.at[g, slot_out],
                zsend.at[g, slot_out],
                zrecv.at[g, slot_out],
                at[way],
            )
        )

    def ring(g, s):
        if s < 4:
            pass_on(g, lax.rem(z + 4 - s, 8), s - 1 if s else None, s, "up")
        if s < 3:
            pass_on(g, lax.rem(z + 5 + s, 8), s + 3 if s else None, s + 4, "down")
        if s == 4:
            low, high = acc[g, z], acc[g, 8 + z]
            for n in (3, 6):
                got = ring_in.at[g, n]
                remote(got, got, zsend.at[g, n], zrecv.at[g, n], at["up"]).wait_recv()
                low += got[0].astype(f32)
                high += got[1].astype(f32)
            acc[g, z] = low
            acc[g, 8 + z] = high
            y_out[g] = acc[g, (1 - yl) * 8 + z].astype(bf16)
            go(remote(y_out.at[g], y_in.at[g], ysend.at[g], yrecv.at[g], at["across"]))

    def finish(g):
        remote(y_out.at[g], y_in.at[g], ysend.at[g], yrecv.at[g], at["across"]).wait_recv()
        total = acc[g, c] + y_in[g].astype(f32)
        if g < 2:
            wg[:, 512 * g : 512 * g + 512] = total
        else:
            ig[...] = total

    act_done(0)
    product(0)
    ring(0, 0)
    relay(2)
    product(1)
    ring(1, 0)
    ring(0, 1)
    ring(1, 1)
    remote(half_out, half_in, tsend.at[0], trecv.at[0], at["core"]).wait_recv()
    pair_out[...] = (part[mine, :] + half_in[...].astype(f32)).astype(bf16)
    go(remote(pair_out, pair_in, tsend.at[1], trecv.at[1], at["far"]))
    ring(0, 2)
    ring(1, 2)

    sums_q = jnp.zeros((256, 16), f32)
    sums_v = jnp.zeros((256, 16), f32)
    sums_u = jnp.zeros((256, 16), f32)
    ends = jnp.zeros((8, 16), f32)
    ones = jnp.ones((8, 128), bf16)
    for g in range(2):
        span = spans(g)
        later, state = states(b_fin, g), states(f_fin, g)
        ex = expand[:, span]
        zs = dot(bs(g), later, COLS) * etx_s[:, span]
        xg = x_ref[:, span].astype(f32)
        xsg = xs_s[:, span].astype(f32)
        dyg = dy_s[:, span].astype(f32)
        zw = z_s[:, span]
        zt = zw + zs
        hg_ref[:, span] = (dtx_s[:, span] * zt + skipx[:, span] * dyg).astype(bf16)
        sums_q += split_left(dyg * y_s[:, span] - xsg * zw, ex, 3, COLS)
        sums_v += split_left(xsg * zs, ex, 2, COLS)
        sums_u += split_left(xg * zt, ex, 2, COLS)
        rows = split_right(ones, state.astype(f32) * later.astype(f32), 2, COLS)
        ends += split_left(rows, ex, 2, COLS)
    triu = jnp.where(iota((256, 256), 0) <= iota((256, 256), 1), 1.0, 0.0).astype(bf16)
    lower = jnp.where(iota((256, 256), 0) > iota((256, 256), 1), 1.0, 0.0).astype(bf16)
    flow = split_right(triu, sums_q, 3) + split_right(lower, sums_v, 3)
    flow = flow + ends[0:1, :] * jnp.exp(last)
    sg_ref[...] = sig * (sums_u - rate * flow)

    act_done(1)
    product(2)
    ring(2, 0)
    ring(0, 3)
    ring(1, 3)
    ring(2, 1)
    remote(pair_out, pair_in, tsend.at[1], trecv.at[1], at["far"]).wait_recv()
    lg[mine, :] = (pair_out[...].astype(f32) + pair_in[...].astype(f32)).astype(bf16)
    go(remote(lg.at[mine], lg.at[mine], tsend.at[2], trecv.at[2], at["core"]))
    ring(2, 2)
    ring(0, 4)
    ring(1, 4)
    ring(2, 3)
    finish(0)
    finish(1)
    ring(2, 4)
    for lane in links.values():
        lane.drain()
    for copy in acts:
        copy.wait_send()
    for e in (f1, f2, b1, b2):
        e[2]()
    finish(2)
    remote(lg.at[other], lg.at[other], tsend.at[2], trecv.at[2], at["core"]).wait_recv()
    for copy in sent:
        copy.wait_send()


def call(x, raw, bias, rate, skip, start, stop, wi, wo, lin, up):
    def vm(shape, kind=bf16):
        return pltpu.VMEM(shape, kind)

    dma = pltpu.SemaphoreType.DMA
    return pl.pallas_call(
        kernel,
        out_shape=(
            jax.ShapeDtypeStruct((256, 2048), bf16),
            jax.ShapeDtypeStruct((256, 1024), bf16),
            jax.ShapeDtypeStruct((256, 16), f32),
            jax.ShapeDtypeStruct((32, 1024), f32),
            jax.ShapeDtypeStruct((32, 512), f32),
        ),
        in_specs=[VM] * 7 + [ANY] * 4,
        out_specs=(VM,) * 5,
        scratch_shapes=[
            vm((2048, 512)), vm((2048, 1024)), vm((256, 2048)), vm((256, 2048)),
            vm((256, 512)), vm((256, 1024)),
            vm((256, 1024), f32), vm((256, 1024), f32),
            vm((256, 1024)), vm((256, 1024)), vm((256, 1024)), vm((256, 1024)),
            vm((256, 1024), f32), vm((256, 1024), f32), vm((256, 1024), f32),
            vm((2, 256, 256), f32), vm((256, 16), f32), vm((16, 256), f32),
            vm((16, 80, 128)), vm((16, 80, 128)), vm((16, 64, 128)), vm((16, 64, 128)),
            vm((16, 64, 128)), vm((16, 64, 128)), vm((16, 64, 128)), vm((16, 64, 128)),
            vm((3, 4, 256, 512)), vm((2, 4, 256, 512)),
            vm((256, 2048), f32), vm((128, 2048)), vm((128, 2048)), vm((128, 2048)), vm((128, 2048)),
            vm((3, 16, 32, 512), f32), vm((3, 7, 2, 32, 512)), vm((3, 7, 2, 32, 512)),
            vm((3, 32, 512)), vm((3, 32, 512)),
            dma((3, 12)), dma((3, 12)), dma((2, 4)), dma((2, 4)), dma((2, 4)), dma((2, 4)),
            dma((4, 16)), dma((4, 16)),
            dma((3, 6)), dma((3, 6)), dma((3, 7)), dma((3, 7)), dma((3,)), dma((3,)), dma((3,)), dma((3,)),
            dma((4,)),
        ],
        compiler_params=pltpu.CompilerParams(
            collective_id=1, has_side_effects=True, vmem_limit_bytes=LIMIT
        ),
        name="whole",
    )(x, raw, bias, rate, skip, start, stop, wi, wo, lin, up)


def per_device(
    layer_in, head_in, step_raw, step_bias, rate_log, skip_gain,
    inject_weight, out_weight, upstream, window_start, lengths,
):
    lg, hg, sg, wg, ig = call(
        head_in[0],
        step_raw[0],
        step_bias[None],
        rate_log[None],
        skip_gain[None],
        window_start[None],
        lengths[None],
        inject_weight.reshape(512, 512),
        out_weight,
        layer_in[0],
        upstream[0],
    )
    return lg[None], hg[None], sg[None], wg, ig.reshape(32, 2, 256)


def solution(mesh):
    placed = (
        P("dp", "ctx", None),
        P("dp", "ctx", "tensor"),
        P("dp", "ctx", "tensor"),
        P("tensor"),
        P("tensor"),
        P("tensor"),
        P("dp", "tensor", None),
        P("dp", "tensor"),
        P("dp", "ctx", None),
        P("dp"),
        P("dp"),
    )
    return jax.shard_map(
        per_device,
        mesh=mesh,
        in_specs=placed,
        out_specs=(
            P("dp", "ctx", None),
            P("dp", "ctx", "tensor"),
            P("dp", "ctx", "tensor"),
            P(("dp", "ctx"), "tensor"),
            P(("dp", "ctx"), "tensor", None),
        ),
        check_vma=False,
    )
```

```python
import jax
import jax.numpy as jnp
from jax import lax
from jax.experimental import pallas as pl
from jax.experimental.pallas import tpu as pltpu
from jax.sharding import PartitionSpec as P

f32 = jnp.float32
bf16 = jnp.bfloat16
MESH = pl.DeviceIdType.MESH
ANY = pl.BlockSpec(memory_space=pl.ANY)
VM = pl.BlockSpec(memory_space=pltpu.VMEM)
WINDOW = 3
LIMIT = 56 * 1024 * 1024
ROWS = (((0,), (0,)), ((), ()))
COLS = (((1,), (1,)), ((), ()))


def remote(src, dst, send, recv, where):
    return pltpu.make_async_remote_copy(
        src_ref=src, dst_ref=dst, send_sem=send, recv_sem=recv, device_id=where, device_id_type=MESH
    )


def greet(partners):
    barrier = pltpu.get_barrier_semaphore()
    for where in partners:
        pl.semaphore_signal(barrier, inc=1, device_id=where, device_id_type=MESH)
    pl.semaphore_wait(barrier, len(partners))


def places():
    x = lax.axis_index("dp")
    c = lax.axis_index("ctx")
    t = lax.axis_index("tensor")
    z = lax.rem(c, 8)
    base = c - z
    spots = dict(
        right={"dp": lax.rem(x + 1, 4)},
        left={"dp": lax.rem(x + 3, 4)},
        up={"ctx": base + lax.rem(z + 1, 8)},
        down={"ctx": base + lax.rem(z + 7, 8)},
        across={"ctx": lax.rem(c + 8, 16)},
        core={"tensor": t + 1 - 2 * lax.rem(t, 2)},
        far={"tensor": lax.rem(t + 2, 4)},
    )
    return x, c, t, z, spots


def dot(a, b, dims=None):
    if dims is None:
        return jnp.dot(a, b, preferred_element_type=f32)
    return lax.dot_general(a, b, dims, preferred_element_type=f32)


def pieces(v, count):
    found = []
    for _ in range(count):
        part = v.astype(bf16)
        found.append(part)
        v = v - part.astype(f32)
    return found


def split_left(v, m, count, dims=None):
    return sum(dot(part, m, dims) for part in pieces(v, count))


def split_right(m, v, count, dims=None):
    return sum(dot(m, part, dims) for part in pieces(v, count))


def iota(shape, axis):
    return lax.broadcasted_iota(jnp.int32, shape, axis)


class Lane:
    def __init__(self, window):
        self.window = window
        self.sent = []
        self.waited = 0

    def push(self, copy):
        while len(self.sent) - self.waited >= self.window:
            self.sent[self.waited].wait_send()
            self.waited += 1
        copy.start()
        self.sent.append(copy)

    def drain(self):
        while self.waited < len(self.sent):
            self.sent[self.waited].wait_send()
            self.waited += 1


def kernel(
    x_ref, raw_ref, bias_ref, rate_ref, skip_ref, start_ref, stop_ref, wi, wo, lin, up,
    lg, hg_ref, sg_ref, wg, ig,
    wi_v, wo_v, lin_v, up_v, proj_s, y_s, z_s, xs_s, xe_s, dy_s, de_s, erx_s, etx_s, dtx_s, ds_s,
    r_s, rt_s, grow_s, w_s, f_out, f_got, f_mid, f_fin, b_out, b_got, b_mid, b_fin,
    factor, act, part, half_out, half_in, pair_out, pair_in, acc, ring_out, ring_in, y_out, y_in,
    wsend, wrecv, asend, arecv, csend, crecv, esend, erecv,
    send, recv, zsend, zrecv, ysend, yrecv, tsend, trecv, local,
):
    x, c, t, z, at = places()
    h = lax.rem(z, 2)
    yl = lax.div(c, 8)
    cr = lax.rem(t, 2)
    lefts, rights, opposite = lax.rem(x + 3, 4), lax.rem(x + 1, 4), lax.rem(x + 2, 4)
    mine = pl.ds(pl.multiple_of(cr * 128, 128), 128)
    other = pl.ds(pl.multiple_of((1 - cr) * 128, 128), 128)

    def quarter(j):
        return pl.ds(pl.multiple_of(j * 512, 512), 512)

    loads = [
        pltpu.make_async_copy(wi, wi_v.at[quarter(x)], local.at[0]),
        pltpu.make_async_copy(wo, wo_v.at[quarter(x)], local.at[1]),
        pltpu.make_async_copy(lin, lin_v, local.at[2]),
        pltpu.make_async_copy(up, up_v, local.at[3]),
    ]
    for load in loads:
        load.start()
    greet(
        [at[k] for k in ("right", "left", "core", "far")]
        + [{"dp": opposite}]
        + [{"ctx": lax.rem(c + k, 16)} for k in range(1, 16)]
    )

    links = {k: Lane(WINDOW) for k in ("right", "left", "up", "down", "across")}
    halves = (h, yl, h)
    relays = (("up", "down"), ("across", "across"), ("up", "down"))

    def strip(ref, g):
        return ref if g == 0 else ref.at[:, 512 * (g - 1) : 512 * g]

    def weight_rows(g, slab, half, q):
        rows = pl.ds(pl.multiple_of(slab * 512 + half * 256 + q * 128, 128), 128)
        return strip(wi_v if g == 0 else wo_v, g).at[rows]

    def first(g, q, event, way):
        rows = pl.ds(pl.multiple_of(halves[g] * 256 + q * 128, 128), 128)
        links[way].push(
            remote(
                strip(wi if g == 0 else wo, g).at[rows],
                weight_rows(g, x, halves[g], q),
                wsend.at[g, event],
                wrecv.at[g, event],
                at[way],
            )
        )

    def arrived(g, slab, half, q, event):
        dst = weight_rows(g, slab, half, q)
        remote(dst, dst, wsend.at[g, event], wrecv.at[g, event], at["left"]).wait_recv()

    def forward(g, slab, q, event, way):
        dst = weight_rows(g, slab, halves[g], q)
        links[way].push(remote(dst, dst, wsend.at[g, event], wrecv.at[g, event], at[way]))

    def slot(g, n):
        h, (first_way, second_way) = halves[g], relays[g]
        if n == 0:
            first(g, 0, 0, "right")
            first(g, 1, 2, "left")
        elif n == 1:
            first(g, 1, 1, "right")
            first(g, 0, 3, "left")
        elif n == 2:
            arrived(g, lefts, h, 0, 0)
            forward(g, lefts, 0, 4, "right")
            arrived(g, rights, h, 1, 2)
            forward(g, rights, 1, 5, "left")
            forward(g, lefts, 0, 6, first_way)
            forward(g, rights, 1, 10, second_way)
        elif n == 3:
            arrived(g, lefts, h, 1, 1)
            forward(g, lefts, 1, 9, second_way)
            arrived(g, rights, h, 0, 3)
            forward(g, rights, 0, 7, first_way)
        else:
            arrived(g, opposite, h, 0, 4)
            forward(g, opposite, 0, 8, first_way)
            arrived(g, opposite, h, 1, 5)
            forward(g, opposite, 1, 11, second_way)

    def gathered(g):
        for n, slab in enumerate((lefts, rights, opposite)):
            arrived(g, slab, 1 - halves[g], 0, 6 + n)
            arrived(g, slab, 1 - halves[g], 1, 9 + n)

    def swap(e, src, dst):
        def to_peer(k):
            to = lax.rem(c + k, 16)
            return remote(src.at[to], dst.at[c], esend.at[e, k], erecv.at[e, k], {"ctx": to})

        def from_peer(k):
            who = lax.rem(c + 16 - k, 16)
            return remote(src.at[who], dst.at[who], esend.at[e, k], erecv.at[e, k], {"ctx": who})

        def each(fn):
            def step(k, carry):
                fn(k)
                return carry

            lax.fori_loop(1, 16, step, 0)

        def begin():
            each(lambda k: to_peer(k).start())
            dst[c] = src[c]

        return (
            begin,
            lambda: each(lambda k: from_peer(k).wait_recv()),
            lambda: each(lambda k: to_peer(k).wait_send()),
        )

    f1 = swap(0, f_out, f_got)
    f2 = swap(1, f_mid, f_fin)
    b1 = swap(2, b_out, b_got)
    b2 = swap(3, b_mid, b_fin)

    slot(0, 0)
    slot(0, 1)

    side16 = iota((16, 1024), 1) - 64 * iota((16, 1024), 0)
    expand = jnp.where((side16 >= 0) & (side16 < 64), 1.0, 0.0).astype(bf16)
    above = iota((256, 256), 0) >= iota((256, 256), 1)
    tril = jnp.where(above, 1.0, 0.0).astype(bf16)
    eye = jnp.where(iota((256, 256), 0) == iota((256, 256), 1), 1.0, 0.0).astype(bf16)
    position = c * 256 + iota((256, 1), 0)
    mask = jnp.where((position >= start_ref[...]) & (position < stop_ref[...]), 1.0, 0.0)
    rate = jnp.exp(rate_ref[...])
    shifted = split_right(eye, raw_ref[...], 3, COLS) + bias_ref[...]
    small = jnp.exp(-jnp.abs(shifted))
    dt = mask * (jnp.maximum(shifted, 0.0) + jnp.log1p(small))
    sig = mask * jnp.where(shifted >= 0.0, 1.0, small) / (1.0 + small)
    running = split_right(tril, -dt * rate, 3)
    r_s[...] = running
    rt = split_left(running, eye, 3, ROWS)
    rt_s[...] = rt
    last = running[255:256, :]
    erx_s[...] = split_left(jnp.exp(running), expand, 2)
    etx_s[...] = split_left(jnp.exp(last - running), expand, 2)
    dtx_s[...] = split_left(dt, expand, 2)
    xs_s[...] = (x_ref[...].astype(f32) * dtx_s[...]).astype(bf16)
    xe_s[...] = (xs_s[...].astype(f32) * etx_s[...]).astype(bf16)
    skipx = split_left(jnp.broadcast_to(skip_ref[...], (8, 16)), expand, 3)[0:1, :]
    decay = jnp.broadcast_to(rt[:, 255:256], (16, 128))
    row = iota((16, 16, 128), 1)
    lines = jnp.zeros((16, 16, 128), f32)
    for n, term in enumerate(pieces(decay, 3)):
        lines = jnp.where(row == n, term.astype(f32)[:, None, :], lines)
    f_out[:, 64:80, :] = lines.astype(bf16)

    slot(0, 2)
    slot(1, 0)
    slot(0, 3)
    slot(1, 1)
    slot(0, 4)
    slot(1, 2)
    slot(2, 0)
    for load in loads:
        load.wait()
    gathered(0)

    def spans(g):
        return slice(512 * g, 512 * g + 512)

    def bs(g):
        return proj_s[:, 256 * g : 256 * g + 128]

    def cs(g):
        return proj_s[:, 256 * g + 128 : 256 * g + 256]

    proj_s[...] = dot(lin_v[...], wi_v[...]).astype(bf16)
    for g in range(2):
        own = dot(xe_s[:, spans(g)], bs(g), ROWS)
        f_out[8 * g : 8 * g + 8, 0:64, :] = own.reshape(8, 64, 128).astype(bf16)
    f1[0]()
    slot(1, 3)
    slot(2, 1)
    slot(1, 4)
    slot(2, 2)
    slot(2, 3)
    slot(2, 4)

    def grow_of(k):
        lines = f_got[k, 64:80, :].astype(f32)
        return jnp.exp(lines[0:1] + lines[1:2] + lines[2:3])

    f1[1]()

    def ahead(k, state):
        f_mid[k] = state.astype(bf16)
        return grow_of(k) * state + f_got[k, 0:64, :].astype(f32)

    lax.fori_loop(0, 16, ahead, jnp.zeros((64, 128), f32))
    f2[0]()

    values = (up_v, lin_v)
    acts = []

    def token_rows(r):
        return pl.ds(pl.multiple_of(r * 64, 64), 64)

    far_t, core_t = lax.rem(t + 2, 4), t + 1 - 2 * cr
    fourth_t = lax.rem(core_t + 2, 4)

    def act_send(n):
        for k in (1, 3, 2):
            to = lax.rem(x + k, 4)
            copy = remote(
                values[n].at[token_rows(t), quarter(to)],
                act.at[n, x, token_rows(t)],
                asend.at[n, k],
                arecv.at[n, k],
                {"dp": to},
            )
            copy.start()
            acts.append(copy)
        act[n, x] = values[n][:, quarter(x)]

    def act_move(n, k, r, event, way):
        dst = act.at[n, lax.rem(x + 4 - k, 4), token_rows(r)]
        return remote(dst, dst, csend.at[n, k, event], crecv.at[n, k, event], at[way])

    def act_share(n):
        for k in (1, 3, 2):
            dst = act.at[n, lax.rem(x + 4 - k, 4), token_rows(t)]
            remote(dst, dst, asend.at[n, k], arecv.at[n, k], at["left"]).wait_recv()
            for event, way in ((0, "far"), (1, "core")):
                copy = act_move(n, k, t, event, way)
                copy.start()
                acts.append(copy)

    def act_pass(n):
        for k in (1, 3, 2):
            act_move(n, k, far_t, 0, "far").wait_recv()
            copy = act_move(n, k, far_t, 2, "core")
            copy.start()
            acts.append(copy)

    def act_done(n):
        for k in (1, 3, 2):
            act_move(n, k, core_t, 1, "core").wait_recv()
            act_move(n, k, fourth_t, 2, "core").wait_recv()

    side = iota((256, 128), 1)
    side16 = iota((256, 16), 1)
    low_side = side < 64

    def half_of(v, half):
        return jnp.where(low_side if half == 0 else ~low_side, v, jnp.zeros_like(v))

    def lanes_of(g, p):
        return pl.ds(pl.multiple_of(512 * g + p * 128, 128), 128)

    def ahead_group(g):
        scores = dot(cs(g), bs(g), COLS)

        def pair(p, carry):
            x2 = xs_s[:, lanes_of(g, p)]
            y2 = jnp.zeros((256, 128), f32)
            for half in range(2):
                head = 8 * g + 2 * p + half
                col = jnp.sum(jnp.where(side16 == head, r_s[...], 0.0), axis=1, keepdims=True)
                line = rt_s[pl.ds(head, 1), :]
                grow = jnp.exp(jnp.where(above, col - line, -1e30))
                w = (scores * grow).astype(bf16)
                grow_s[head] = grow
                w_s[head] = w
                y2 += dot(w, half_of(x2, half))
            y_s[:, lanes_of(g, p)] = y2
            return carry

        lax.fori_loop(0, 4, pair, 0)

    def back_group(g):
        ds_s[g] = jnp.zeros((256, 256), f32)

        def pair(p, carry):
            x2 = xs_s[:, lanes_of(g, p)]
            dy2 = dy_s[:, lanes_of(g, p)]
            z2 = jnp.zeros((256, 128), f32)
            ds = ds_s[g]
            for half in range(2):
                head = 8 * g + 2 * p + half
                dm = half_of(dy2, half)
                z2 += dot(w_s[head], dm, ROWS)
                ds += dot(dm, half_of(x2, half), COLS) * grow_s[head]
            z_s[:, lanes_of(g, p)] = z2
            ds_s[g] = ds
            return carry

        lax.fori_loop(0, 4, pair, 0)

    act_send(0)
    act_send(1)
    ahead_group(0)
    ahead_group(1)
    gathered(1)
    dy_s[:, 0:512] = (dot(up_v[...], wo_v[:, 0:512]).astype(bf16).astype(f32) * mask).astype(bf16)
    gathered(2)
    dy_s[:, 512:] = (dot(up_v[...], wo_v[:, 512:]).astype(bf16).astype(f32) * mask).astype(bf16)
    de_s[...] = (dy_s[...].astype(f32) * erx_s[...]).astype(bf16)
    for g in range(2):
        pull = dot(de_s[:, spans(g)], cs(g), ROWS)
        b_out[8 * g : 8 * g + 8] = pull.reshape(8, 64, 128).astype(bf16)
    b1[0]()

    def states(fin, g):
        return fin[8 * g : 8 * g + 8].reshape(512, 128)

    sent = []

    def go(copy):
        copy.start()
        sent.append(copy)

    def own_send(g):
        rows = [pl.ds(0, 128), pl.ds(128, 128)]
        for q, event, way in ((0, 0, "right"), (1, 2, "left"), (1, 1, "right"), (0, 3, "left")):
            src = factor.at[g, x, rows[q]]
            go(remote(src, src, send.at[g, event], recv.at[g, event], at[way]))

    def came(g, slab, q, event):
        dst = factor.at[g, slab, pl.ds(128 * q, 128)]
        remote(dst, dst, send.at[g, event], recv.at[g, event], at["left"]).wait_recv()
        return dst

    def relay(g):
        src = came(g, lefts, 0, 0)
        go(remote(src, src, send.at[g, 4], recv.at[g, 4], at["right"]))
        src = came(g, rights, 1, 2)
        go(remote(src, src, send.at[g, 5], recv.at[g, 5], at["left"]))

    f2[1]()
    for g in range(2):
        span = spans(g)
        ya = dot(cs(g), states(f_fin, g), COLS) * erx_s[:, span]
        yt = y_s[:, span] + ya
        y_s[:, span] = yt
        value = mask * (yt + skipx[:, span] * x_ref[:, span].astype(f32))
        factor[g, x] = value.astype(bf16)
        own_send(g)
    act_share(0)
    act_share(1)
    back_group(0)
    back_group(1)

    b1[1]()

    def behind(n, state):
        k = 15 - n
        b_mid[k] = state.astype(bf16)
        return grow_of(k) * state + b_got[k].astype(f32)

    lax.fori_loop(0, 16, behind, jnp.zeros((64, 128), f32))
    b2[0]()
    act_pass(0)
    act_pass(1)
    relay(0)
    relay(1)
    b2[1]()

    for g in range(2):
        later = states(b_fin, g)
        state = states(f_fin, g)
        dsr = ds_s[g].astype(bf16)
        db = dot(dsr, cs(g), ROWS) + dot(xe_s[:, spans(g)], later)
        dc = dot(dsr, bs(g)) + dot(de_s[:, spans(g)], state)
        factor[2, x, :, 256 * g : 256 * g + 128] = db.astype(bf16)
        factor[2, x, :, 256 * g + 128 : 256 * g + 256] = dc.astype(bf16)
    own_send(2)
    part[...] = dot(factor[2, x], wi_v[...], COLS)
    half_out[...] = part[other, :].astype(bf16)
    go(remote(half_out, half_in, tsend.at[0], trecv.at[0], at["core"]))

    def product(g):
        came(g, lefts, 1, 1)
        came(g, rights, 0, 3)
        came(g, opposite, 0, 4)
        came(g, opposite, 1, 5)
        a = act[0 if g < 2 else 1].reshape(1024, 512)
        acc[g] = dot(a, factor[g].reshape(1024, 512), ROWS).reshape(16, 32, 512)

    def pass_on(g, k, slot_in, slot_out, way):
        low, high = acc[g, k], acc[g, 8 + k]
        if slot_in is not None:
            got = ring_in.at[g, slot_in]
            remote(got, got, zsend.at[g, slot_in], zrecv.at[g, slot_in], at["up"]).wait_recv()
            low += got[0].astype(f32)
            high += got[1].astype(f32)
        ring_out[g, slot_out, 0] = low.astype(bf16)
        ring_out[g, slot_out, 1] = high.astype(bf16)
        go(
            remote(
                ring_out.at[g, slot_out],
                ring_in.at[g, slot_out],
                zsend.at[g, slot_out],
                zrecv.at[g, slot_out],
                at[way],
            )
        )

    def ring(g, s):
        if s < 4:
            pass_on(g, lax.rem(z + 4 - s, 8), s - 1 if s else None, s, "up")
        if s < 3:
            pass_on(g, lax.rem(z + 5 + s, 8), s + 3 if s else None, s + 4, "down")
        if s == 4:
            low, high = acc[g, z], acc[g, 8 + z]
            for n in (3, 6):
                got = ring_in.at[g, n]
                remote(got, got, zsend.at[g, n], zrecv.at[g, n], at["up"]).wait_recv()
                low += got[0].astype(f32)
                high += got[1].astype(f32)
            acc[g, z] = low
            acc[g, 8 + z] = high
            y_out[g] = acc[g, (1 - yl) * 8 + z].astype(bf16)
            go(remote(y_out.at[g], y_in.at[g], ysend.at[g], yrecv.at[g], at["across"]))

    def finish(g):
        remote(y_out.at[g], y_in.at[g], ysend.at[g], yrecv.at[g], at["across"]).wait_recv()
        total = acc[g, c] + y_in[g].astype(f32)
        if g < 2:
            wg[:, 512 * g : 512 * g + 512] = total
        else:
            ig[:, 0, :] = total[:, 0:256]
            ig[:, 1, :] = total[:, 256:512]

    act_done(0)
    product(0)
    ring(0, 0)
    relay(2)
    product(1)
    ring(1, 0)
    ring(0, 1)
    ring(1, 1)
    remote(half_out, half_in, tsend.at[0], trecv.at[0], at["core"]).wait_recv()
    pair_out[...] = (part[mine, :] + half_in[...].astype(f32)).astype(bf16)
    go(remote(pair_out, pair_in, tsend.at[1], trecv.at[1], at["far"]))
    ring(0, 2)
    ring(1, 2)

    sums_q = jnp.zeros((256, 16), f32)
    sums_v = jnp.zeros((256, 16), f32)
    sums_u = jnp.zeros((256, 16), f32)
    ends = jnp.zeros((8, 16), f32)
    ones = jnp.ones((8, 128), bf16)
    for g in range(2):
        span = spans(g)
        later, state = states(b_fin, g), states(f_fin, g)
        ex = expand[:, span]
        zs = dot(bs(g), later, COLS) * etx_s[:, span]
        xg = x_ref[:, span].astype(f32)
        xsg = xs_s[:, span].astype(f32)
        dyg = dy_s[:, span].astype(f32)
        zw = z_s[:, span]
        zt = zw + zs
        hg_ref[:, span] = (dtx_s[:, span] * zt + skipx[:, span] * dyg).astype(bf16)
        sums_q += split_left(dyg * y_s[:, span] - xsg * zw, ex, 3, COLS)
        sums_v += split_left(xsg * zs, ex, 2, COLS)
        sums_u += split_left(xg * zt, ex, 2, COLS)
        rows = split_right(ones, state.astype(f32) * later.astype(f32), 2, COLS)
        ends += split_left(rows, ex, 2, COLS)
    triu = jnp.where(iota((256, 256), 0) <= iota((256, 256), 1), 1.0, 0.0).astype(bf16)
    lower = jnp.where(iota((256, 256), 0) > iota((256, 256), 1), 1.0, 0.0).astype(bf16)
    flow = split_right(triu, sums_q, 3) + split_right(lower, sums_v, 3)
    flow = flow + ends[0:1, :] * jnp.exp(last)
    sg_ref[...] = sig * (sums_u - rate * flow)

    act_done(1)
    product(2)
    ring(2, 0)
    ring(0, 3)
    ring(1, 3)
    ring(2, 1)
    remote(pair_out, pair_in, tsend.at[1], trecv.at[1], at["far"]).wait_recv()
    lg[mine, :] = (pair_out[...].astype(f32) + pair_in[...].astype(f32)).astype(bf16)
    go(remote(lg.at[mine], lg.at[mine], tsend.at[2], trecv.at[2], at["core"]))
    ring(2, 2)
    ring(0, 4)
    ring(1, 4)
    ring(2, 3)
    finish(0)
    finish(1)
    ring(2, 4)
    for lane in links.values():
        lane.drain()
    for copy in acts:
        copy.wait_send()
    for e in (f1, f2, b1, b2):
        e[2]()
    finish(2)
    remote(lg.at[other], lg.at[other], tsend.at[2], trecv.at[2], at["core"]).wait_recv()
    for copy in sent:
        copy.wait_send()


def call(x, raw, bias, rate, skip, start, stop, wi, wo, lin, up):
    def vm(shape, kind=bf16):
        return pltpu.VMEM(shape, kind)

    dma = pltpu.SemaphoreType.DMA
    return pl.pallas_call(
        kernel,
        out_shape=(
            jax.ShapeDtypeStruct((256, 2048), bf16),
            jax.ShapeDtypeStruct((256, 1024), bf16),
            jax.ShapeDtypeStruct((256, 16), f32),
            jax.ShapeDtypeStruct((32, 1024), f32),
            jax.ShapeDtypeStruct((32, 2, 256), f32),
        ),
        in_specs=[VM] * 7 + [ANY] * 4,
        out_specs=(VM,) * 5,
        scratch_shapes=[
            vm((2048, 512)), vm((2048, 1024)), vm((256, 2048)), vm((256, 2048)),
            vm((256, 512)), vm((256, 1024), f32), vm((256, 1024), f32),
            vm((256, 1024)), vm((256, 1024)), vm((256, 1024)), vm((256, 1024)),
            vm((256, 1024), f32), vm((256, 1024), f32), vm((256, 1024), f32),
            vm((2, 256, 256), f32), vm((256, 16), f32), vm((16, 256), f32), vm((16, 256, 256), f32), vm((16, 256, 256)),
            vm((16, 80, 128)), vm((16, 80, 128)), vm((16, 64, 128)), vm((16, 64, 128)),
            vm((16, 64, 128)), vm((16, 64, 128)), vm((16, 64, 128)), vm((16, 64, 128)),
            vm((3, 4, 256, 512)), vm((2, 4, 256, 512)),
            vm((256, 2048), f32), vm((128, 2048)), vm((128, 2048)), vm((128, 2048)), vm((128, 2048)),
            vm((3, 16, 32, 512), f32), vm((3, 7, 2, 32, 512)), vm((3, 7, 2, 32, 512)),
            vm((3, 32, 512)), vm((3, 32, 512)),
            dma((3, 12)), dma((3, 12)), dma((2, 4)), dma((2, 4)), dma((2, 4, 3)), dma((2, 4, 3)),
            dma((4, 16)), dma((4, 16)),
            dma((3, 6)), dma((3, 6)), dma((3, 7)), dma((3, 7)), dma((3,)), dma((3,)), dma((3,)), dma((3,)),
            dma((4,)),
        ],
        compiler_params=pltpu.CompilerParams(
            collective_id=1, has_side_effects=True, vmem_limit_bytes=LIMIT
        ),
        name="whole",
    )(x, raw, bias, rate, skip, start, stop, wi, wo, lin, up)


def per_device(
    layer_in, head_in, step_raw, step_bias, rate_log, skip_gain,
    inject_weight, out_weight, upstream, window_start, lengths,
):
    lg, hg, sg, wg, ig = call(
        head_in[0],
        step_raw[0].T,
        step_bias[None],
        rate_log[None],
        skip_gain[None],
        window_start[None],
        lengths[None],
        inject_weight.reshape(512, 512),
        out_weight,
        layer_in[0],
        upstream[0],
    )
    return lg[None], hg[None], sg[None], wg, ig


def solution(mesh):
    placed = (
        P("dp", "ctx", None),
        P("dp", "ctx", "tensor"),
        P("dp", "ctx", "tensor"),
        P("tensor"),
        P("tensor"),
        P("tensor"),
        P("dp", "tensor", None),
        P("dp", "tensor"),
        P("dp", "ctx", None),
        P("dp"),
        P("dp"),
    )
    return jax.shard_map(
        per_device,
        mesh=mesh,
        in_specs=placed,
        out_specs=(
            P("dp", "ctx", None),
            P("dp", "ctx", "tensor"),
            P("dp", "ctx", "tensor"),
            P(("dp", "ctx"), "tensor"),
            P(("dp", "ctx"), "tensor", None),
        ),
        check_vma=False,
    )
```

```python
import jax
import jax.numpy as jnp
from jax import lax
from jax.experimental import pallas as pl
from jax.experimental.pallas import tpu as pltpu
from jax.sharding import PartitionSpec as P

f32 = jnp.float32
bf16 = jnp.bfloat16
MESH = pl.DeviceIdType.MESH
ANY = pl.BlockSpec(memory_space=pl.ANY)
VM = pl.BlockSpec(memory_space=pltpu.VMEM)
WINDOW = 3
LIMIT = 56 * 1024 * 1024
ROWS = (((0,), (0,)), ((), ()))
COLS = (((1,), (1,)), ((), ()))


def remote(src, dst, send, recv, where):
    return pltpu.make_async_remote_copy(
        src_ref=src, dst_ref=dst, send_sem=send, recv_sem=recv, device_id=where, device_id_type=MESH
    )


def greet(partners):
    barrier = pltpu.get_barrier_semaphore()
    for where in partners:
        pl.semaphore_signal(barrier, inc=1, device_id=where, device_id_type=MESH)
    pl.semaphore_wait(barrier, len(partners))


def places():
    x = lax.axis_index("dp")
    c = lax.axis_index("ctx")
    t = lax.axis_index("tensor")
    z = lax.rem(c, 8)
    base = c - z
    spots = dict(
        right={"dp": lax.rem(x + 1, 4)},
        left={"dp": lax.rem(x + 3, 4)},
        up={"ctx": base + lax.rem(z + 1, 8)},
        down={"ctx": base + lax.rem(z + 7, 8)},
        across={"ctx": lax.rem(c + 8, 16)},
        core={"tensor": t + 1 - 2 * lax.rem(t, 2)},
        far={"tensor": lax.rem(t + 2, 4)},
    )
    return x, c, t, z, spots


def dot(a, b, dims=None):
    if dims is None:
        return jnp.dot(a, b, preferred_element_type=f32)
    return lax.dot_general(a, b, dims, preferred_element_type=f32)


def pieces(v, count):
    found = []
    for _ in range(count):
        part = v.astype(bf16)
        found.append(part)
        v = v - part.astype(f32)
    return found


def split_left(v, m, count, dims=None):
    return sum(dot(part, m, dims) for part in pieces(v, count))


def split_right(m, v, count, dims=None):
    return sum(dot(m, part, dims) for part in pieces(v, count))


def iota(shape, axis):
    return lax.broadcasted_iota(jnp.int32, shape, axis)


class Lane:
    def __init__(self, window):
        self.window = window
        self.sent = []
        self.waited = 0

    def push(self, copy):
        while len(self.sent) - self.waited >= self.window:
            self.sent[self.waited].wait_send()
            self.waited += 1
        copy.start()
        self.sent.append(copy)

    def drain(self):
        while self.waited < len(self.sent):
            self.sent[self.waited].wait_send()
            self.waited += 1


def kernel(
    x_ref, raw_ref, bias_ref, rate_ref, skip_ref, start_ref, stop_ref, wi, wo, lin, up,
    lg, hg_ref, sg_ref, wg, ig,
    wi_v, wo_v, lin_v, up_v, proj_s, y_s, z_s, xs_s, xe_s, dy_s, de_s, erx_s, etx_s, dtx_s, ds_s,
    r_s, rt_s, grow_s, w_s, f_out, f_got, f_mid, f_fin, b_out, b_got, b_mid, b_fin,
    factor, act, part, half_out, half_in, pair_out, pair_in, acc, ring_out, ring_in, y_out, y_in,
    wsend, wrecv, asend, arecv, csend, crecv, esend, erecv,
    send, recv, zsend, zrecv, ysend, yrecv, tsend, trecv, local,
):
    x, c, t, z, at = places()
    h = lax.rem(z, 2)
    yl = lax.div(c, 8)
    cr = lax.rem(t, 2)
    lefts, rights, opposite = lax.rem(x + 3, 4), lax.rem(x + 1, 4), lax.rem(x + 2, 4)
    mine = pl.ds(pl.multiple_of(cr * 128, 128), 128)
    other = pl.ds(pl.multiple_of((1 - cr) * 128, 128), 128)

    def quarter(j):
        return pl.ds(pl.multiple_of(j * 512, 512), 512)

    loads = [
        pltpu.make_async_copy(wi, wi_v.at[quarter(x)], local.at[0]),
        pltpu.make_async_copy(wo, wo_v.at[quarter(x)], local.at[1]),
        pltpu.make_async_copy(lin, lin_v, local.at[2]),
        pltpu.make_async_copy(up, up_v, local.at[3]),
    ]
    for load in loads:
        load.start()
    greet(
        [at[k] for k in ("right", "left", "core", "far")]
        + [{"dp": opposite}]
        + [{"ctx": lax.rem(c + k, 16)} for k in range(1, 16)]
    )

    links = {k: Lane(WINDOW) for k in ("right", "left", "up", "down", "across")}
    halves = (h, yl, h)
    relays = (("up", "down"), ("across", "across"), ("up", "down"))

    def strip(ref, g):
        return ref if g == 0 else ref.at[:, 512 * (g - 1) : 512 * g]

    def weight_rows(g, slab, half, q):
        rows = pl.ds(pl.multiple_of(slab * 512 + half * 256 + q * 128, 128), 128)
        return strip(wi_v if g == 0 else wo_v, g).at[rows]

    def first(g, q, event, way):
        rows = pl.ds(pl.multiple_of(halves[g] * 256 + q * 128, 128), 128)
        links[way].push(
            remote(
                strip(wi if g == 0 else wo, g).at[rows],
                weight_rows(g, x, halves[g], q),
                wsend.at[g, event],
                wrecv.at[g, event],
                at[way],
            )
        )

    def arrived(g, slab, half, q, event):
        dst = weight_rows(g, slab, half, q)
        remote(dst, dst, wsend.at[g, event], wrecv.at[g, event], at["left"]).wait_recv()

    def forward(g, slab, q, event, way):
        dst = weight_rows(g, slab, halves[g], q)
        links[way].push(remote(dst, dst, wsend.at[g, event], wrecv.at[g, event], at[way]))

    def slot(g, n):
        h, (first_way, second_way) = halves[g], relays[g]
        if n == 0:
            first(g, 0, 0, "right")
            first(g, 1, 2, "left")
        elif n == 1:
            first(g, 1, 1, "right")
            first(g, 0, 3, "left")
        elif n == 2:
            arrived(g, lefts, h, 0, 0)
            forward(g, lefts, 0, 4, "right")
            arrived(g, rights, h, 1, 2)
            forward(g, rights, 1, 5, "left")
            forward(g, lefts, 0, 6, first_way)
            forward(g, rights, 1, 10, second_way)
        elif n == 3:
            arrived(g, lefts, h, 1, 1)
            forward(g, lefts, 1, 9, second_way)
            arrived(g, rights, h, 0, 3)
            forward(g, rights, 0, 7, first_way)
        else:
            arrived(g, opposite, h, 0, 4)
            forward(g, opposite, 0, 8, first_way)
            arrived(g, opposite, h, 1, 5)
            forward(g, opposite, 1, 11, second_way)

    def gathered(g):
        for n, slab in enumerate((lefts, rights, opposite)):
            arrived(g, slab, 1 - halves[g], 0, 6 + n)
            arrived(g, slab, 1 - halves[g], 1, 9 + n)

    def swap(e, src, dst):
        def to_peer(k):
            to = lax.rem(c + k, 16)
            return remote(src.at[to], dst.at[c], esend.at[e, k], erecv.at[e, k], {"ctx": to})

        def from_peer(k):
            who = lax.rem(c + 16 - k, 16)
            return remote(src.at[who], dst.at[who], esend.at[e, k], erecv.at[e, k], {"ctx": who})

        def each(fn):
            def step(k, carry):
                fn(k)
                return carry

            lax.fori_loop(1, 16, step, 0)

        def begin():
            each(lambda k: to_peer(k).start())
            dst[c] = src[c]

        return (
            begin,
            lambda: each(lambda k: from_peer(k).wait_recv()),
            lambda: each(lambda k: to_peer(k).wait_send()),
        )

    f1 = swap(0, f_out, f_got)
    f2 = swap(1, f_mid, f_fin)
    b1 = swap(2, b_out, b_got)
    b2 = swap(3, b_mid, b_fin)

    slot(0, 0)
    slot(0, 1)

    side16 = iota((16, 1024), 1) - 64 * iota((16, 1024), 0)
    expand = jnp.where((side16 >= 0) & (side16 < 64), 1.0, 0.0).astype(bf16)
    above = iota((256, 256), 0) >= iota((256, 256), 1)
    tril = jnp.where(above, 1.0, 0.0).astype(bf16)
    eye = jnp.where(iota((256, 256), 0) == iota((256, 256), 1), 1.0, 0.0).astype(bf16)
    position = c * 256 + iota((256, 1), 0)
    mask = jnp.where((position >= start_ref[...]) & (position < stop_ref[...]), 1.0, 0.0)
    rate = jnp.exp(rate_ref[...])
    shifted = split_right(eye, raw_ref[...], 3, COLS) + bias_ref[...]
    small = jnp.exp(-jnp.abs(shifted))
    dt = mask * (jnp.maximum(shifted, 0.0) + jnp.log1p(small))
    sig = mask * jnp.where(shifted >= 0.0, 1.0, small) / (1.0 + small)
    running = split_right(tril, -dt * rate, 3)
    r_s[...] = running
    rt = split_left(running, eye, 3, ROWS)
    rt_s[...] = rt
    last = running[255:256, :]
    erx_s[...] = split_left(jnp.exp(running), expand, 2)
    etx_s[...] = split_left(jnp.exp(last - running), expand, 2)
    dtx_s[...] = split_left(dt, expand, 2)
    xs_s[...] = (x_ref[...].astype(f32) * dtx_s[...]).astype(bf16)
    xe_s[...] = (xs_s[...].astype(f32) * etx_s[...]).astype(bf16)
    skipx = split_left(jnp.broadcast_to(skip_ref[...], (8, 16)), expand, 3)[0:1, :]
    decay = jnp.broadcast_to(rt[:, 255:256], (16, 128))
    row = iota((16, 16, 128), 1)
    lines = jnp.zeros((16, 16, 128), f32)
    for n, term in enumerate(pieces(decay, 3)):
        lines = jnp.where(row == n, term.astype(f32)[:, None, :], lines)
    f_out[:, 64:80, :] = lines.astype(bf16)

    slot(0, 2)
    slot(1, 0)
    slot(0, 3)
    slot(1, 1)
    slot(0, 4)
    slot(1, 2)
    slot(2, 0)
    for load in loads:
        load.wait()
    gathered(0)

    def spans(g):
        return slice(512 * g, 512 * g + 512)

    def bs(g):
        return proj_s[:, 256 * g : 256 * g + 128]

    def cs(g):
        return proj_s[:, 256 * g + 128 : 256 * g + 256]

    proj_s[...] = dot(lin_v[...], wi_v[...]).astype(bf16)
    for g in range(2):
        own = dot(xe_s[:, spans(g)], bs(g), ROWS)
        f_out[8 * g : 8 * g + 8, 0:64, :] = own.reshape(8, 64, 128).astype(bf16)
    f1[0]()
    slot(1, 3)
    slot(2, 1)
    slot(1, 4)
    slot(2, 2)
    slot(2, 3)
    slot(2, 4)

    def grow_of(k):
        lines = f_got[k, 64:80, :].astype(f32)
        return jnp.exp(lines[0:1] + lines[1:2] + lines[2:3])

    f1[1]()

    def ahead(k, state):
        f_mid[k] = state.astype(bf16)
        return grow_of(k) * state + f_got[k, 0:64, :].astype(f32)

    lax.fori_loop(0, 16, ahead, jnp.zeros((64, 128), f32))
    f2[0]()

    values = (up_v, lin_v)
    acts = []

    def token_rows(r):
        return pl.ds(pl.multiple_of(r * 64, 64), 64)

    far_t, core_t = lax.rem(t + 2, 4), t + 1 - 2 * cr
    fourth_t = lax.rem(core_t + 2, 4)

    def act_send(n):
        for k in (1, 3, 2):
            to = lax.rem(x + k, 4)
            copy = remote(
                values[n].at[token_rows(t), quarter(to)],
                act.at[n, x, token_rows(t)],
                asend.at[n, k],
                arecv.at[n, k],
                {"dp": to},
            )
            copy.start()
            acts.append(copy)
        act[n, x] = values[n][:, quarter(x)]

    def act_move(n, k, r, event, way):
        dst = act.at[n, lax.rem(x + 4 - k, 4), token_rows(r)]
        return remote(dst, dst, csend.at[n, k, event], crecv.at[n, k, event], at[way])

    def act_share(n):
        for k in (1, 3, 2):
            dst = act.at[n, lax.rem(x + 4 - k, 4), token_rows(t)]
            remote(dst, dst, asend.at[n, k], arecv.at[n, k], at["left"]).wait_recv()
            for event, way in ((0, "far"), (1, "core")):
                copy = act_move(n, k, t, event, way)
                copy.start()
                acts.append(copy)

    def act_pass(n):
        for k in (1, 3, 2):
            act_move(n, k, far_t, 0, "far").wait_recv()
            copy = act_move(n, k, far_t, 2, "core")
            copy.start()
            acts.append(copy)

    def act_done(n):
        for k in (1, 3, 2):
            act_move(n, k, core_t, 1, "core").wait_recv()
            act_move(n, k, fourth_t, 2, "core").wait_recv()

    side = iota((256, 128), 1)
    side16 = iota((256, 16), 1)
    low_side = side < 64

    def half_of(v, half):
        return jnp.where(low_side if half == 0 else ~low_side, v, jnp.zeros_like(v))

    def lanes_of(g, p):
        return pl.ds(pl.multiple_of(512 * g + p * 128, 128), 128)

    def ahead_group(g):
        scores = dot(cs(g), bs(g), COLS)

        def pair(p, carry):
            x2 = xs_s[:, lanes_of(g, p)]
            y2 = jnp.zeros((256, 128), f32)
            for half in range(2):
                head = 8 * g + 2 * p + half
                col = jnp.sum(jnp.where(side16 == head, r_s[...], 0.0), axis=1, keepdims=True)
                line = rt_s[pl.ds(head, 1), :]
                grow = jnp.exp(jnp.where(above, col - line, -1e30))
                w = (scores * grow).astype(bf16)
                grow_s[head] = grow
                w_s[head] = w
                y2 += dot(w, half_of(x2, half))
            y_s[:, lanes_of(g, p)] = y2
            return carry

        lax.fori_loop(0, 4, pair, 0)

    def back_group(g):
        ds_s[g] = jnp.zeros((256, 256), f32)

        def pair(p, carry):
            x2 = xs_s[:, lanes_of(g, p)]
            dy2 = dy_s[:, lanes_of(g, p)]
            z2 = jnp.zeros((256, 128), f32)
            ds = ds_s[g]
            for half in range(2):
                head = 8 * g + 2 * p + half
                dm = half_of(dy2, half)
                z2 += dot(w_s[head], dm, ROWS)
                ds += dot(dm, half_of(x2, half), COLS) * grow_s[head]
            z_s[:, lanes_of(g, p)] = z2
            ds_s[g] = ds
            return carry

        lax.fori_loop(0, 4, pair, 0)

    act_send(0)
    act_send(1)
    ahead_group(0)
    ahead_group(1)
    gathered(1)
    dy_s[:, 0:512] = (dot(up_v[...], wo_v[:, 0:512]).astype(bf16).astype(f32) * mask).astype(bf16)
    gathered(2)
    dy_s[:, 512:] = (dot(up_v[...], wo_v[:, 512:]).astype(bf16).astype(f32) * mask).astype(bf16)
    de_s[...] = (dy_s[...].astype(f32) * erx_s[...]).astype(bf16)
    for g in range(2):
        pull = dot(de_s[:, spans(g)], cs(g), ROWS)
        b_out[8 * g : 8 * g + 8] = pull.reshape(8, 64, 128).astype(bf16)
    b1[0]()

    def states(fin, g):
        return fin[8 * g : 8 * g + 8].reshape(512, 128)

    sent = []

    def go(copy):
        copy.start()
        sent.append(copy)

    def view(ref, g, *index):
        if g < 2:
            return ref.at[(g,) + index]
        tail = (slice(None),) * (len(ref.shape) - 2 - len(index))
        return ref.at[(2,) + index + tail + (slice(256 * g - 512, 256 * g - 256),)]

    def rows_of(g, slab, q):
        rows = pl.ds(128 * q, 128)
        if g < 2:
            return factor.at[g, slab, rows]
        return factor.at[2, slab, rows, 256 * g - 512 : 256 * g - 256]

    def own_send(g):
        for q, event, way in ((0, 0, "right"), (1, 2, "left"), (1, 1, "right"), (0, 3, "left")):
            src = rows_of(g, x, q)
            go(remote(src, src, send.at[g, event], recv.at[g, event], at[way]))

    def came(g, slab, q, event):
        dst = rows_of(g, slab, q)
        remote(dst, dst, send.at[g, event], recv.at[g, event], at["left"]).wait_recv()
        return dst

    def relay(g):
        src = came(g, lefts, 0, 0)
        go(remote(src, src, send.at[g, 4], recv.at[g, 4], at["right"]))
        src = came(g, rights, 1, 2)
        go(remote(src, src, send.at[g, 5], recv.at[g, 5], at["left"]))

    f2[1]()
    for g in range(2):
        span = spans(g)
        ya = dot(cs(g), states(f_fin, g), COLS) * erx_s[:, span]
        yt = y_s[:, span] + ya
        y_s[:, span] = yt
        value = mask * (yt + skipx[:, span] * x_ref[:, span].astype(f32))
        factor[g, x] = value.astype(bf16)
        own_send(g)
    act_share(0)
    act_share(1)
    back_group(0)
    back_group(1)

    b1[1]()

    def behind(n, state):
        k = 15 - n
        b_mid[k] = state.astype(bf16)
        return grow_of(k) * state + b_got[k].astype(f32)

    lax.fori_loop(0, 16, behind, jnp.zeros((64, 128), f32))
    b2[0]()
    act_pass(0)
    act_pass(1)
    relay(0)
    relay(1)
    b2[1]()

    for g in range(2):
        later = states(b_fin, g)
        state = states(f_fin, g)
        dsr = ds_s[g].astype(bf16)
        db = dot(dsr, cs(g), ROWS) + dot(xe_s[:, spans(g)], later)
        dc = dot(dsr, bs(g)) + dot(de_s[:, spans(g)], state)
        factor[2, x, :, 256 * g : 256 * g + 128] = db.astype(bf16)
        factor[2, x, :, 256 * g + 128 : 256 * g + 256] = dc.astype(bf16)
        own_send(2 + g)
    part[...] = dot(factor[2, x], wi_v[...], COLS)
    half_out[...] = part[other, :].astype(bf16)
    go(remote(half_out, half_in, tsend.at[0], trecv.at[0], at["core"]))

    def product(g):
        came(g, lefts, 1, 1)
        came(g, rights, 0, 3)
        came(g, opposite, 0, 4)
        came(g, opposite, 1, 5)
        a = act[0 if g < 2 else 1].reshape(1024, 512)
        if g < 2:
            acc[g] = dot(a, factor[g].reshape(1024, 512), ROWS).reshape(16, 32, 512)
        else:
            lanes = slice(256 * g - 512, 256 * g - 256)
            right = factor[2, :, :, lanes].reshape(1024, 256)
            acc[2, :, :, lanes] = dot(a, right, ROWS).reshape(16, 32, 256)

    def arrival(g, n):
        got = view(ring_in, g, n)
        remote(got, got, zsend.at[g, n], zrecv.at[g, n], at["up"]).wait_recv()
        return got[0].astype(f32), got[1].astype(f32)

    def pass_on(g, k, slot_in, slot_out, way):
        low, high = view(acc, g, k)[...], view(acc, g, 8 + k)[...]
        if slot_in is not None:
            more = arrival(g, slot_in)
            low += more[0]
            high += more[1]
        src, dst = view(ring_out, g, slot_out), view(ring_in, g, slot_out)
        src[0] = low.astype(bf16)
        src[1] = high.astype(bf16)
        go(remote(src, dst, zsend.at[g, slot_out], zrecv.at[g, slot_out], at[way]))

    def ring(g, s):
        if s < 4:
            pass_on(g, lax.rem(z + 4 - s, 8), s - 1 if s else None, s, "up")
        if s < 3:
            pass_on(g, lax.rem(z + 5 + s, 8), s + 3 if s else None, s + 4, "down")
        if s == 4:
            low, high = view(acc, g, z)[...], view(acc, g, 8 + z)[...]
            for n in (3, 6):
                more = arrival(g, n)
                low += more[0]
                high += more[1]
            view(acc, g, z)[...] = low
            view(acc, g, 8 + z)[...] = high
            src, dst = view(y_out, g), view(y_in, g)
            src[...] = view(acc, g, (1 - yl) * 8 + z)[...].astype(bf16)
            go(remote(src, dst, ysend.at[g], yrecv.at[g], at["across"]))

    def finish(g):
        src, dst = view(y_out, g), view(y_in, g)
        remote(src, dst, ysend.at[g], yrecv.at[g], at["across"]).wait_recv()
        total = view(acc, g, c)[...] + dst[...].astype(f32)
        if g < 2:
            wg[:, 512 * g : 512 * g + 512] = total
        else:
            ig[:, 256 * g - 512 : 256 * g - 256] = total

    sums_q = jnp.zeros((256, 16), f32)
    sums_v = jnp.zeros((256, 16), f32)
    sums_u = jnp.zeros((256, 16), f32)
    ends = jnp.zeros((8, 16), f32)
    sums = (sums_q, sums_v, sums_u, ends)
    ones = jnp.ones((8, 128), bf16)
    def rest(g, sums):
        sums_q, sums_v, sums_u, ends = sums
        span = spans(g)
        later, state = states(b_fin, g), states(f_fin, g)
        ex = expand[:, span]
        zs = dot(bs(g), later, COLS) * etx_s[:, span]
        xg = x_ref[:, span].astype(f32)
        xsg = xs_s[:, span].astype(f32)
        dyg = dy_s[:, span].astype(f32)
        zw = z_s[:, span]
        zt = zw + zs
        hg_ref[:, span] = (dtx_s[:, span] * zt + skipx[:, span] * dyg).astype(bf16)
        sums_q += split_left(dyg * y_s[:, span] - xsg * zw, ex, 3, COLS)
        sums_v += split_left(xsg * zs, ex, 2, COLS)
        sums_u += split_left(xg * zt, ex, 2, COLS)
        rows = split_right(ones, state.astype(f32) * later.astype(f32), 2, COLS)
        ends += split_left(rows, ex, 2, COLS)
        return sums_q, sums_v, sums_u, ends

    act_done(0)
    product(0)
    ring(0, 0)
    relay(2)
    product(1)
    ring(1, 0)
    ring(0, 1)
    relay(3)
    ring(1, 1)
    remote(half_out, half_in, tsend.at[0], trecv.at[0], at["core"]).wait_recv()
    pair_out[...] = (part[mine, :] + half_in[...].astype(f32)).astype(bf16)
    go(remote(pair_out, pair_in, tsend.at[1], trecv.at[1], at["far"]))
    act_done(1)
    product(2)
    ring(2, 0)
    ring(0, 2)
    ring(1, 2)
    sums = rest(0, sums)
    product(3)
    ring(3, 0)
    ring(2, 1)
    ring(0, 3)
    ring(1, 3)
    ring(3, 1)
    ring(2, 2)
    sums = rest(1, sums)
    ring(3, 2)
    ring(2, 3)
    ring(0, 4)
    ring(1, 4)
    ring(3, 3)
    remote(pair_out, pair_in, tsend.at[1], trecv.at[1], at["far"]).wait_recv()
    lg[mine, :] = (pair_out[...].astype(f32) + pair_in[...].astype(f32)).astype(bf16)
    go(remote(lg.at[mine], lg.at[mine], tsend.at[2], trecv.at[2], at["core"]))
    ring(2, 4)
    ring(3, 4)
    sums_q, sums_v, sums_u, ends = sums
    triu = jnp.where(iota((256, 256), 0) <= iota((256, 256), 1), 1.0, 0.0).astype(bf16)
    lower = jnp.where(iota((256, 256), 0) > iota((256, 256), 1), 1.0, 0.0).astype(bf16)
    flow = split_right(triu, sums_q, 3) + split_right(lower, sums_v, 3)
    flow = flow + ends[0:1, :] * jnp.exp(last)
    sg_ref[...] = sig * (sums_u - rate * flow)

    finish(0)
    finish(1)
    for lane in links.values():
        lane.drain()
    for copy in acts:
        copy.wait_send()
    for e in (f1, f2, b1, b2):
        e[2]()
    finish(2)
    finish(3)
    remote(lg.at[other], lg.at[other], tsend.at[2], trecv.at[2], at["core"]).wait_recv()
    for copy in sent:
        copy.wait_send()


def whole(x, raw, bias, rate, skip, start, stop, wi, wo, lin, up):
    def vm(shape, kind=bf16):
        return pltpu.VMEM(shape, kind)

    dma = pltpu.SemaphoreType.DMA
    return pl.pallas_call(
        kernel,
        out_shape=(
            jax.ShapeDtypeStruct((256, 2048), bf16),
            jax.ShapeDtypeStruct((256, 1024), bf16),
            jax.ShapeDtypeStruct((256, 16), f32),
            jax.ShapeDtypeStruct((32, 1024), f32),
            jax.ShapeDtypeStruct((32, 512), f32),
        ),
        in_specs=[VM] * 7 + [ANY] * 4,
        out_specs=(VM,) * 5,
        scratch_shapes=[
            vm((2048, 512)), vm((2048, 1024)), vm((256, 2048)), vm((256, 2048)),
            vm((256, 512)), vm((256, 1024), f32), vm((256, 1024), f32),
            vm((256, 1024)), vm((256, 1024)), vm((256, 1024)), vm((256, 1024)),
            vm((256, 1024), f32), vm((256, 1024), f32), vm((256, 1024), f32),
            vm((2, 256, 256), f32), vm((256, 16), f32), vm((16, 256), f32), vm((16, 256, 256), f32), vm((16, 256, 256)),
            vm((16, 80, 128)), vm((16, 80, 128)), vm((16, 64, 128)), vm((16, 64, 128)),
            vm((16, 64, 128)), vm((16, 64, 128)), vm((16, 64, 128)), vm((16, 64, 128)),
            vm((3, 4, 256, 512)), vm((2, 4, 256, 512)),
            vm((256, 2048), f32), vm((128, 2048)), vm((128, 2048)), vm((128, 2048)), vm((128, 2048)),
            vm((3, 16, 32, 512), f32), vm((3, 7, 2, 32, 512)), vm((3, 7, 2, 32, 512)),
            vm((3, 32, 512)), vm((3, 32, 512)),
            dma((3, 12)), dma((3, 12)), dma((2, 4)), dma((2, 4)), dma((2, 4, 3)), dma((2, 4, 3)),
            dma((4, 16)), dma((4, 16)),
            dma((4, 6)), dma((4, 6)), dma((4, 7)), dma((4, 7)), dma((4,)), dma((4,)), dma((3,)), dma((3,)),
            dma((4,)),
        ],
        compiler_params=pltpu.CompilerParams(
            collective_id=1, has_side_effects=True, vmem_limit_bytes=LIMIT
        ),
        name="whole",
    )(x, raw, bias, rate, skip, start, stop, wi, wo, lin, up)


def settle_kernel(lg, hg, sg, wg, ig, lg_out, hg_out, sg_out, wg_out, ig_out):
    lg_out[...] = lg[...]
    hg_out[...] = hg[...]
    sg_out[...] = sg[...]
    wg_out[...] = wg[...]
    ig_out[:, 0, :] = ig[:, 0:256]
    ig_out[:, 1, :] = ig[:, 256:512]


def settle(*found):
    shapes = [(v.shape, v.dtype) for v in found[:4]] + [((32, 2, 256), f32)]
    return pl.pallas_call(
        settle_kernel,
        out_shape=tuple(jax.ShapeDtypeStruct(*kind) for kind in shapes),
        in_specs=[VM] * 5,
        out_specs=(VM,) * 5,
        name="settle",
    )(*found)


def call(*inputs):
    return settle(*whole(*inputs))


def per_device(
    layer_in, head_in, step_raw, step_bias, rate_log, skip_gain,
    inject_weight, out_weight, upstream, window_start, lengths,
):
    lg, hg, sg, wg, ig = call(
        head_in[0],
        step_raw[0].T,
        step_bias[None],
        rate_log[None],
        skip_gain[None],
        window_start[None],
        lengths[None],
        inject_weight.reshape(512, 512),
        out_weight,
        layer_in[0],
        upstream[0],
    )
    return lg[None], hg[None], sg[None], wg, ig


def solution(mesh):
    placed = (
        P("dp", "ctx", None),
        P("dp", "ctx", "tensor"),
        P("dp", "ctx", "tensor"),
        P("tensor"),
        P("tensor"),
        P("tensor"),
        P("dp", "tensor", None),
        P("dp", "tensor"),
        P("dp", "ctx", None),
        P("dp"),
        P("dp"),
    )
    return jax.shard_map(
        per_device,
        mesh=mesh,
        in_specs=placed,
        out_specs=(
            P("dp", "ctx", None),
            P("dp", "ctx", "tensor"),
            P("dp", "ctx", "tensor"),
            P(("dp", "ctx"), "tensor"),
            P(("dp", "ctx"), "tensor", None),
        ),
        check_vma=False,
    )
```

```python
import jax
import jax.numpy as jnp
from jax import lax
from jax.experimental import pallas as pl
from jax.experimental.pallas import tpu as pltpu
from jax.sharding import PartitionSpec as P

f32 = jnp.float32
bf16 = jnp.bfloat16
MESH = pl.DeviceIdType.MESH
ANY = pl.BlockSpec(memory_space=pl.ANY)
VM = pl.BlockSpec(memory_space=pltpu.VMEM)
WINDOW = 3
LIMIT = 56 * 1024 * 1024
ROWS = (((0,), (0,)), ((), ()))
COLS = (((1,), (1,)), ((), ()))


def remote(src, dst, send, recv, where):
    return pltpu.make_async_remote_copy(
        src_ref=src, dst_ref=dst, send_sem=send, recv_sem=recv, device_id=where, device_id_type=MESH
    )


def greet(partners):
    barrier = pltpu.get_barrier_semaphore()
    for where in partners:
        pl.semaphore_signal(barrier, inc=1, device_id=where, device_id_type=MESH)
    pl.semaphore_wait(barrier, len(partners))


def places():
    x = lax.axis_index("dp")
    c = lax.axis_index("ctx")
    t = lax.axis_index("tensor")
    z = lax.rem(c, 8)
    base = c - z
    spots = dict(
        right={"dp": lax.rem(x + 1, 4)},
        left={"dp": lax.rem(x + 3, 4)},
        up={"ctx": base + lax.rem(z + 1, 8)},
        down={"ctx": base + lax.rem(z + 7, 8)},
        across={"ctx": lax.rem(c + 8, 16)},
        core={"tensor": t + 1 - 2 * lax.rem(t, 2)},
        far={"tensor": lax.rem(t + 2, 4)},
    )
    return x, c, t, z, spots


def dot(a, b, dims=None):
    if dims is None:
        return jnp.dot(a, b, preferred_element_type=f32)
    return lax.dot_general(a, b, dims, preferred_element_type=f32)


def pieces(v, count):
    found = []
    for _ in range(count):
        part = v.astype(bf16)
        found.append(part)
        v = v - part.astype(f32)
    return found


def split_left(v, m, count, dims=None):
    return sum(dot(part, m, dims) for part in pieces(v, count))


def split_right(m, v, count, dims=None):
    return sum(dot(m, part, dims) for part in pieces(v, count))


def iota(shape, axis):
    return lax.broadcasted_iota(jnp.int32, shape, axis)


class Lane:
    def __init__(self, window):
        self.window = window
        self.sent = []
        self.waited = 0

    def push(self, copy):
        while len(self.sent) - self.waited >= self.window:
            self.sent[self.waited].wait_send()
            self.waited += 1
        copy.start()
        self.sent.append(copy)

    def drain(self):
        while self.waited < len(self.sent):
            self.sent[self.waited].wait_send()
            self.waited += 1


def kernel(
    x_ref, raw_ref, bias_ref, rate_ref, skip_ref, start_ref, stop_ref, wi, wo, lin, up,
    lg, hg_ref, sg_ref, wg, ig,
    wi_v, wo_v, lin_v, up_v, proj_s, y_s, z_s, xs_s, xe_s, dy_s, de_s, erx_s, etx_s, dtx_s, ds_s,
    r_s, rt_s, grow_s, w_s, f_out, f_got, f_mid, f_fin, b_out, b_got, b_mid, b_fin,
    factor, act, part, half_out, half_in, pair_out, pair_in, acc, ring_out, ring_in, y_out, y_in, d_out, d_got,
    wsend, wrecv, asend, arecv, csend, crecv, esend, erecv,
    send, recv, zsend, zrecv, ysend, yrecv, tsend, trecv, local,
):
    x, c, t, z, at = places()
    h = lax.rem(z, 2)
    yl = lax.div(c, 8)
    cr = lax.rem(t, 2)
    lefts, rights, opposite = lax.rem(x + 3, 4), lax.rem(x + 1, 4), lax.rem(x + 2, 4)
    mine = pl.ds(pl.multiple_of(cr * 128, 128), 128)
    other = pl.ds(pl.multiple_of((1 - cr) * 128, 128), 128)

    def quarter(j):
        return pl.ds(pl.multiple_of(j * 512, 512), 512)

    loads = [
        pltpu.make_async_copy(wi, wi_v.at[quarter(x)], local.at[0]),
        pltpu.make_async_copy(wo, wo_v.at[quarter(x)], local.at[1]),
        pltpu.make_async_copy(lin, lin_v, local.at[2]),
        pltpu.make_async_copy(up, up_v, local.at[3]),
    ]
    for load in loads:
        load.start()
    greet(
        [at[k] for k in ("right", "left", "core", "far")]
        + [{"dp": opposite}]
        + [{"ctx": lax.rem(c + k, 16)} for k in range(1, 16)]
    )

    links = {k: Lane(WINDOW) for k in ("right", "left", "up", "down", "across")}
    halves = (h, yl, h)
    relays = (("up", "down"), ("across", "across"), ("up", "down"))

    def strip(ref, g):
        return ref if g == 0 else ref.at[:, 512 * (g - 1) : 512 * g]

    def weight_rows(g, slab, half, q):
        rows = pl.ds(pl.multiple_of(slab * 512 + half * 256 + q * 128, 128), 128)
        return strip(wi_v if g == 0 else wo_v, g).at[rows]

    def first(g, q, event, way):
        rows = pl.ds(pl.multiple_of(halves[g] * 256 + q * 128, 128), 128)
        links[way].push(
            remote(
                strip(wi if g == 0 else wo, g).at[rows],
                weight_rows(g, x, halves[g], q),
                wsend.at[g, event],
                wrecv.at[g, event],
                at[way],
            )
        )

    def arrived(g, slab, half, q, event):
        dst = weight_rows(g, slab, half, q)
        remote(dst, dst, wsend.at[g, event], wrecv.at[g, event], at["left"]).wait_recv()

    def forward(g, slab, q, event, way):
        dst = weight_rows(g, slab, halves[g], q)
        links[way].push(remote(dst, dst, wsend.at[g, event], wrecv.at[g, event], at[way]))

    def slot(g, n):
        h, (first_way, second_way) = halves[g], relays[g]
        if n == 0:
            first(g, 0, 0, "right")
            first(g, 1, 2, "left")
        elif n == 1:
            first(g, 1, 1, "right")
            first(g, 0, 3, "left")
        elif n == 2:
            arrived(g, lefts, h, 0, 0)
            forward(g, lefts, 0, 4, "right")
            arrived(g, rights, h, 1, 2)
            forward(g, rights, 1, 5, "left")
            forward(g, lefts, 0, 6, first_way)
            forward(g, rights, 1, 10, second_way)
        elif n == 3:
            arrived(g, lefts, h, 1, 1)
            forward(g, lefts, 1, 9, second_way)
            arrived(g, rights, h, 0, 3)
            forward(g, rights, 0, 7, first_way)
        else:
            arrived(g, opposite, h, 0, 4)
            forward(g, opposite, 0, 8, first_way)
            arrived(g, opposite, h, 1, 5)
            forward(g, opposite, 1, 11, second_way)

    def gathered(g):
        for n, slab in enumerate((lefts, rights, opposite)):
            arrived(g, slab, 1 - halves[g], 0, 6 + n)
            arrived(g, slab, 1 - halves[g], 1, 9 + n)

    def swap(e, src, dst):
        def to_peer(k):
            to = lax.rem(c + k, 16)
            return remote(src.at[to], dst.at[c], esend.at[e, k], erecv.at[e, k], {"ctx": to})

        def from_peer(k):
            who = lax.rem(c + 16 - k, 16)
            return remote(src.at[who], dst.at[who], esend.at[e, k], erecv.at[e, k], {"ctx": who})

        def each(fn):
            def step(k, carry):
                fn(k)
                return carry

            lax.fori_loop(1, 16, step, 0, unroll=True)

        def begin():
            each(lambda k: to_peer(k).start())
            dst[c] = src[c]

        return (
            begin,
            lambda: each(lambda k: from_peer(k).wait_recv()),
            lambda: each(lambda k: to_peer(k).wait_send()),
        )

    f1 = swap(0, f_out, f_got)
    f2 = swap(1, f_mid, f_fin)
    b1 = swap(2, b_out, b_got)
    b2 = swap(3, b_mid, b_fin)
    sums_out = {2: swap(4, d_out.at[0], d_got.at[0]), 3: swap(5, d_out.at[1], d_got.at[1])}

    slot(0, 0)
    slot(0, 1)

    side16 = iota((16, 1024), 1) - 64 * iota((16, 1024), 0)
    expand = jnp.where((side16 >= 0) & (side16 < 64), 1.0, 0.0).astype(bf16)
    above = iota((256, 256), 0) >= iota((256, 256), 1)
    tril = jnp.where(above, 1.0, 0.0).astype(bf16)
    eye = jnp.where(iota((256, 256), 0) == iota((256, 256), 1), 1.0, 0.0).astype(bf16)
    position = c * 256 + iota((256, 1), 0)
    mask = jnp.where((position >= start_ref[...]) & (position < stop_ref[...]), 1.0, 0.0)
    rate = jnp.exp(rate_ref[...])
    shifted = split_right(eye, raw_ref[...], 3, COLS) + bias_ref[...]
    small = jnp.exp(-jnp.abs(shifted))
    dt = mask * (jnp.maximum(shifted, 0.0) + jnp.log1p(small))
    sig = mask * jnp.where(shifted >= 0.0, 1.0, small) / (1.0 + small)
    running = split_right(tril, -dt * rate, 3)
    r_s[...] = running
    rt = split_left(running, eye, 3, ROWS)
    rt_s[...] = rt
    last = running[255:256, :]
    erx_s[...] = split_left(jnp.exp(running), expand, 2)
    etx_s[...] = split_left(jnp.exp(last - running), expand, 2)
    dtx_s[...] = split_left(dt, expand, 2)
    xs_s[...] = (x_ref[...].astype(f32) * dtx_s[...]).astype(bf16)
    xe_s[...] = (xs_s[...].astype(f32) * etx_s[...]).astype(bf16)
    skipx = split_left(jnp.broadcast_to(skip_ref[...], (8, 16)), expand, 3)[0:1, :]
    decay = jnp.broadcast_to(rt[:, 255:256], (16, 128))
    row = iota((16, 16, 128), 1)
    lines = jnp.zeros((16, 16, 128), f32)
    for n, term in enumerate(pieces(decay, 3)):
        lines = jnp.where(row == n, term.astype(f32)[:, None, :], lines)
    f_out[:, 64:80, :] = lines.astype(bf16)

    slot(0, 2)
    slot(1, 0)
    slot(0, 3)
    slot(1, 1)
    slot(0, 4)
    slot(1, 2)
    slot(2, 0)
    for load in loads:
        load.wait()
    gathered(0)

    def spans(g):
        return slice(512 * g, 512 * g + 512)

    def bs(g):
        return proj_s[:, 256 * g : 256 * g + 128]

    def cs(g):
        return proj_s[:, 256 * g + 128 : 256 * g + 256]

    proj_s[...] = dot(lin_v[...], wi_v[...]).astype(bf16)
    for g in range(2):
        own = dot(xe_s[:, spans(g)], bs(g), ROWS)
        f_out[8 * g : 8 * g + 8, 0:64, :] = own.reshape(8, 64, 128).astype(bf16)
    f1[0]()
    slot(1, 3)
    slot(2, 1)
    slot(1, 4)
    slot(2, 2)
    slot(2, 3)

    def grow_of(k):
        lines = f_got[k, 64:80, :].astype(f32)
        return jnp.exp(lines[0:1] + lines[1:2] + lines[2:3])

    f1[1]()

    def ahead(k, state):
        f_mid[k] = state.astype(bf16)
        return grow_of(k) * state + f_got[k, 0:64, :].astype(f32)

    lax.fori_loop(0, 16, ahead, jnp.zeros((64, 128), f32), unroll=True)
    f2[0]()
    slot(2, 4)

    values = (up_v, lin_v)
    acts = []

    def token_rows(r):
        return pl.ds(pl.multiple_of(r * 64, 64), 64)

    far_t, core_t = lax.rem(t + 2, 4), t + 1 - 2 * cr
    fourth_t = lax.rem(core_t + 2, 4)

    def act_send(n):
        for k in (1, 3, 2):
            to = lax.rem(x + k, 4)
            copy = remote(
                values[n].at[token_rows(t), quarter(to)],
                act.at[n, x, token_rows(t)],
                asend.at[n, k],
                arecv.at[n, k],
                {"dp": to},
            )
            copy.start()
            acts.append(copy)
        act[n, x] = values[n][:, quarter(x)]

    def act_move(n, k, r, event, way):
        dst = act.at[n, lax.rem(x + 4 - k, 4), token_rows(r)]
        return remote(dst, dst, csend.at[n, k, event], crecv.at[n, k, event], at[way])

    def act_share(n):
        for k in (1, 3, 2):
            dst = act.at[n, lax.rem(x + 4 - k, 4), token_rows(t)]
            remote(dst, dst, asend.at[n, k], arecv.at[n, k], at["left"]).wait_recv()
            for event, way in ((0, "far"), (1, "core")):
                copy = act_move(n, k, t, event, way)
                copy.start()
                acts.append(copy)

    def act_pass(n):
        for k in (1, 3, 2):
            act_move(n, k, far_t, 0, "far").wait_recv()
            copy = act_move(n, k, far_t, 2, "core")
            copy.start()
            acts.append(copy)

    def act_done(n):
        for k in (1, 3, 2):
            act_move(n, k, core_t, 1, "core").wait_recv()
            act_move(n, k, fourth_t, 2, "core").wait_recv()

    side = iota((256, 128), 1)
    side16 = iota((256, 16), 1)
    low_side = side < 64

    def half_of(v, half):
        return jnp.where(low_side if half == 0 else ~low_side, v, jnp.zeros_like(v))

    def lanes_of(g, p):
        return pl.ds(pl.multiple_of(512 * g + p * 128, 128), 128)

    def ahead_group(g):
        scores = dot(cs(g), bs(g), COLS)

        def pair(p, carry):
            x2 = xs_s[:, lanes_of(g, p)]
            y2 = jnp.zeros((256, 128), f32)
            for half in range(2):
                head = 8 * g + 2 * p + half
                col = jnp.sum(jnp.where(side16 == head, r_s[...], 0.0), axis=1, keepdims=True)
                line = rt_s[pl.ds(head, 1), :]
                grow = jnp.exp(jnp.where(above, col - line, -1e30))
                w = (scores * grow).astype(bf16)
                grow_s[head] = grow
                w_s[head] = w
                y2 += dot(w, half_of(x2, half))
            y_s[:, lanes_of(g, p)] = y2
            return carry

        lax.fori_loop(0, 4, pair, 0)

    def back_group(g):
        ds_s[g] = jnp.zeros((256, 256), f32)

        def pair(p, carry):
            x2 = xs_s[:, lanes_of(g, p)]
            dy2 = dy_s[:, lanes_of(g, p)]
            z2 = jnp.zeros((256, 128), f32)
            ds = ds_s[g]
            for half in range(2):
                head = 8 * g + 2 * p + half
                dm = half_of(dy2, half)
                z2 += dot(w_s[head], dm, ROWS)
                ds += dot(dm, half_of(x2, half), COLS) * grow_s[head]
            z_s[:, lanes_of(g, p)] = z2
            ds_s[g] = ds
            return carry

        lax.fori_loop(0, 4, pair, 0)

    act_send(0)
    act_send(1)
    ahead_group(0)
    ahead_group(1)
    gathered(1)
    dy_s[:, 0:512] = (dot(up_v[...], wo_v[:, 0:512]).astype(bf16).astype(f32) * mask).astype(bf16)
    def states(fin, g):
        return fin[8 * g : 8 * g + 8].reshape(512, 128)

    sent = []

    def go(copy):
        copy.start()
        sent.append(copy)

    def view(ref, g, *index):
        if g < 2:
            return ref.at[(g,) + index]
        tail = (slice(None),) * (len(ref.shape) - 2 - len(index))
        return ref.at[(2,) + index + tail + (slice(256 * g - 512, 256 * g - 256),)]

    def rows_of(g, slab, q):
        rows = pl.ds(128 * q, 128)
        if g < 2:
            return factor.at[g, slab, rows]
        return factor.at[2, slab, rows, 256 * g - 512 : 256 * g - 256]

    def own_send(g):
        for q, event, way in ((0, 0, "right"), (1, 2, "left"), (1, 1, "right"), (0, 3, "left")):
            src = rows_of(g, x, q)
            go(remote(src, src, send.at[g, event], recv.at[g, event], at[way]))

    def came(g, slab, q, event):
        dst = rows_of(g, slab, q)
        remote(dst, dst, send.at[g, event], recv.at[g, event], at["left"]).wait_recv()
        return dst

    def relay(g):
        src = came(g, lefts, 0, 0)
        go(remote(src, src, send.at[g, 4], recv.at[g, 4], at["right"]))
        src = came(g, rights, 1, 2)
        go(remote(src, src, send.at[g, 5], recv.at[g, 5], at["left"]))

    f2[1]()
    for g in range(2):
        span = spans(g)
        ya = dot(cs(g), states(f_fin, g), COLS) * erx_s[:, span]
        yt = y_s[:, span] + ya
        y_s[:, span] = yt
        value = mask * (yt + skipx[:, span] * x_ref[:, span].astype(f32))
        factor[g, x] = value.astype(bf16)
        own_send(g)
    gathered(2)
    dy_s[:, 512:] = (dot(up_v[...], wo_v[:, 512:]).astype(bf16).astype(f32) * mask).astype(bf16)
    de_s[...] = (dy_s[...].astype(f32) * erx_s[...]).astype(bf16)
    for g in range(2):
        pull = dot(de_s[:, spans(g)], cs(g), ROWS)
        b_out[8 * g : 8 * g + 8] = pull.reshape(8, 64, 128).astype(bf16)
    b1[0]()

    act_share(0)
    act_share(1)
    back_group(0)
    back_group(1)

    b1[1]()

    def behind(n, state):
        k = 15 - n
        b_mid[k] = state.astype(bf16)
        return grow_of(k) * state + b_got[k].astype(f32)

    lax.fori_loop(0, 16, behind, jnp.zeros((64, 128), f32), unroll=True)
    b2[0]()
    act_pass(0)
    act_pass(1)
    relay(0)
    relay(1)
    b2[1]()

    for g in range(2):
        later = states(b_fin, g)
        state = states(f_fin, g)
        dsr = ds_s[g].astype(bf16)
        db = dot(dsr, cs(g), ROWS) + dot(xe_s[:, spans(g)], later)
        dc = dot(dsr, bs(g)) + dot(de_s[:, spans(g)], state)
        factor[2, x, :, 256 * g : 256 * g + 128] = db.astype(bf16)
        factor[2, x, :, 256 * g + 128 : 256 * g + 256] = dc.astype(bf16)
        own_send(2 + g)
    part[...] = dot(factor[2, x], wi_v[...], COLS)
    half_out[...] = part[other, :].astype(bf16)
    go(remote(half_out, half_in, tsend.at[0], trecv.at[0], at["core"]))

    def product(g):
        came(g, lefts, 1, 1)
        came(g, rights, 0, 3)
        came(g, opposite, 0, 4)
        came(g, opposite, 1, 5)
        a = act[0 if g < 2 else 1].reshape(1024, 512)
        if g < 2:
            acc[g] = dot(a, factor[g].reshape(1024, 512), ROWS).reshape(16, 32, 512)
        else:
            lanes = slice(256 * g - 512, 256 * g - 256)
            right = factor[2, :, :, lanes].reshape(1024, 256)
            acc[2, :, :, lanes] = dot(a, right, ROWS).reshape(16, 32, 256)

    def arrival(g, n):
        got = view(ring_in, g, n)
        remote(got, got, zsend.at[g, n], zrecv.at[g, n], at["up"]).wait_recv()
        return got[0].astype(f32), got[1].astype(f32)

    def pass_on(g, k, slot_in, slot_out, way):
        low, high = view(acc, g, k)[...], view(acc, g, 8 + k)[...]
        if slot_in is not None:
            more = arrival(g, slot_in)
            low += more[0]
            high += more[1]
        src, dst = view(ring_out, g, slot_out), view(ring_in, g, slot_out)
        src[0] = low.astype(bf16)
        src[1] = high.astype(bf16)
        go(remote(src, dst, zsend.at[g, slot_out], zrecv.at[g, slot_out], at[way]))

    def ring(g, s):
        if s < 4:
            pass_on(g, lax.rem(z + 4 - s, 8), s - 1 if s else None, s, "up")
        if s < 3:
            pass_on(g, lax.rem(z + 5 + s, 8), s + 3 if s else None, s + 4, "down")
        if s == 4:
            low, high = view(acc, g, z)[...], view(acc, g, 8 + z)[...]
            for n in (3, 6):
                more = arrival(g, n)
                low += more[0]
                high += more[1]
            view(acc, g, z)[...] = low
            view(acc, g, 8 + z)[...] = high
            src, dst = view(y_out, g), view(y_in, g)
            src[...] = view(acc, g, (1 - yl) * 8 + z)[...].astype(bf16)
            go(remote(src, dst, ysend.at[g], yrecv.at[g], at["across"]))

    def finish(g):
        src, dst = view(y_out, g), view(y_in, g)
        remote(src, dst, ysend.at[g], yrecv.at[g], at["across"]).wait_recv()
        total = view(acc, g, c)[...] + dst[...].astype(f32)
        if g < 2:
            wg[:, 512 * g : 512 * g + 512] = total
        else:
            ig[:, 256 * g - 512 : 256 * g - 256] = total

    sums_q = jnp.zeros((256, 16), f32)
    sums_v = jnp.zeros((256, 16), f32)
    sums_u = jnp.zeros((256, 16), f32)
    ends = jnp.zeros((8, 16), f32)
    sums = (sums_q, sums_v, sums_u, ends)
    ones = jnp.ones((8, 128), bf16)
    def rest(g, sums):
        sums_q, sums_v, sums_u, ends = sums
        span = spans(g)
        later, state = states(b_fin, g), states(f_fin, g)
        ex = expand[:, span]
        zs = dot(bs(g), later, COLS) * etx_s[:, span]
        xg = x_ref[:, span].astype(f32)
        xsg = xs_s[:, span].astype(f32)
        dyg = dy_s[:, span].astype(f32)
        zw = z_s[:, span]
        zt = zw + zs
        hg_ref[:, span] = (dtx_s[:, span] * zt + skipx[:, span] * dyg).astype(bf16)
        sums_q += split_left(dyg * y_s[:, span] - xsg * zw, ex, 3, COLS)
        sums_v += split_left(xsg * zs, ex, 2, COLS)
        sums_u += split_left(xg * zt, ex, 2, COLS)
        rows = split_right(ones, state.astype(f32) * later.astype(f32), 2, COLS)
        ends += split_left(rows, ex, 2, COLS)
        return sums_q, sums_v, sums_u, ends

    act_done(0)
    product(0)
    ring(0, 0)
    relay(2)
    product(1)
    ring(1, 0)
    ring(0, 1)
    relay(3)
    ring(1, 1)
    remote(half_out, half_in, tsend.at[0], trecv.at[0], at["core"]).wait_recv()
    pair_out[...] = (part[mine, :] + half_in[...].astype(f32)).astype(bf16)
    go(remote(pair_out, pair_in, tsend.at[1], trecv.at[1], at["far"]))
    act_done(1)
    product(2)
    d_out[0] = view(acc, 2)[...].astype(bf16)
    sums_out[2][0]()
    ring(0, 2)
    ring(1, 2)
    sums = rest(0, sums)
    product(3)
    d_out[1] = view(acc, 3)[...].astype(bf16)
    sums_out[3][0]()
    ring(0, 3)
    ring(1, 3)
    sums = rest(1, sums)
    ring(0, 4)
    ring(1, 4)
    remote(pair_out, pair_in, tsend.at[1], trecv.at[1], at["far"]).wait_recv()
    lg[mine, :] = (pair_out[...].astype(f32) + pair_in[...].astype(f32)).astype(bf16)
    go(remote(lg.at[mine], lg.at[mine], tsend.at[2], trecv.at[2], at["core"]))
    sums_q, sums_v, sums_u, ends = sums
    triu = jnp.where(iota((256, 256), 0) <= iota((256, 256), 1), 1.0, 0.0).astype(bf16)
    lower = jnp.where(iota((256, 256), 0) > iota((256, 256), 1), 1.0, 0.0).astype(bf16)
    flow = split_right(triu, sums_q, 3) + split_right(lower, sums_v, 3)
    flow = flow + ends[0:1, :] * jnp.exp(last)
    sg_ref[...] = sig * (sums_u - rate * flow)

    finish(0)
    finish(1)
    for lane in links.values():
        lane.drain()
    for copy in acts:
        copy.wait_send()
    for e in (f1, f2, b1, b2):
        e[2]()
    sums_out[2][1]()
    sums_out[2][2]()
    ig[:, 0:256] = jnp.sum(d_got[0].astype(f32), axis=0)
    sums_out[3][1]()
    sums_out[3][2]()
    ig[:, 256:512] = jnp.sum(d_got[1].astype(f32), axis=0)
    remote(lg.at[other], lg.at[other], tsend.at[2], trecv.at[2], at["core"]).wait_recv()
    for copy in sent:
        copy.wait_send()


def whole(x, raw, bias, rate, skip, start, stop, wi, wo, lin, up):
    def vm(shape, kind=bf16):
        return pltpu.VMEM(shape, kind)

    dma = pltpu.SemaphoreType.DMA
    return pl.pallas_call(
        kernel,
        out_shape=(
            jax.ShapeDtypeStruct((256, 2048), bf16),
            jax.ShapeDtypeStruct((256, 1024), bf16),
            jax.ShapeDtypeStruct((256, 16), f32),
            jax.ShapeDtypeStruct((32, 1024), f32),
            jax.ShapeDtypeStruct((32, 512), f32),
        ),
        in_specs=[VM] * 7 + [ANY] * 4,
        out_specs=(VM,) * 5,
        scratch_shapes=[
            vm((2048, 512)), vm((2048, 1024)), vm((256, 2048)), vm((256, 2048)),
            vm((256, 512)), vm((256, 1024), f32), vm((256, 1024), f32),
            vm((256, 1024)), vm((256, 1024)), vm((256, 1024)), vm((256, 1024)),
            vm((256, 1024), f32), vm((256, 1024), f32), vm((256, 1024), f32),
            vm((2, 256, 256), f32), vm((256, 16), f32), vm((16, 256), f32), vm((16, 256, 256), f32), vm((16, 256, 256)),
            vm((16, 80, 128)), vm((16, 80, 128)), vm((16, 64, 128)), vm((16, 64, 128)),
            vm((16, 64, 128)), vm((16, 64, 128)), vm((16, 64, 128)), vm((16, 64, 128)),
            vm((3, 4, 256, 512)), vm((2, 4, 256, 512)),
            vm((256, 2048), f32), vm((128, 2048)), vm((128, 2048)), vm((128, 2048)), vm((128, 2048)),
            vm((3, 16, 32, 512), f32), vm((3, 7, 2, 32, 512)), vm((3, 7, 2, 32, 512)),
            vm((3, 32, 512)), vm((3, 32, 512)), vm((2, 16, 32, 256)), vm((2, 16, 32, 256)),
            dma((3, 12)), dma((3, 12)), dma((2, 4)), dma((2, 4)), dma((2, 4, 3)), dma((2, 4, 3)),
            dma((6, 16)), dma((6, 16)),
            dma((4, 6)), dma((4, 6)), dma((4, 7)), dma((4, 7)), dma((4,)), dma((4,)), dma((3,)), dma((3,)),
            dma((4,)),
        ],
        compiler_params=pltpu.CompilerParams(
            collective_id=1, has_side_effects=True, vmem_limit_bytes=LIMIT
        ),
        name="whole",
    )(x, raw, bias, rate, skip, start, stop, wi, wo, lin, up)


def settle_kernel(lg, hg, sg, wg, ig, lg_out, hg_out, sg_out, wg_out, ig_out):
    lg_out[...] = lg[...]
    hg_out[...] = hg[...]
    sg_out[...] = sg[...]
    wg_out[...] = wg[...]
    ig_out[:, 0, :] = ig[:, 0:256]
    ig_out[:, 1, :] = ig[:, 256:512]


def settle(*found):
    shapes = [(v.shape, v.dtype) for v in found[:4]] + [((32, 2, 256), f32)]
    return pl.pallas_call(
        settle_kernel,
        out_shape=tuple(jax.ShapeDtypeStruct(*kind) for kind in shapes),
        in_specs=[VM] * 5,
        out_specs=(VM,) * 5,
        name="settle",
    )(*found)


def call(*inputs):
    return settle(*whole(*inputs))


def per_device(
    layer_in, head_in, step_raw, step_bias, rate_log, skip_gain,
    inject_weight, out_weight, upstream, window_start, lengths,
):
    lg, hg, sg, wg, ig = call(
        head_in[0],
        step_raw[0].T,
        step_bias[None],
        rate_log[None],
        skip_gain[None],
        window_start[None],
        lengths[None],
        inject_weight.reshape(512, 512),
        out_weight,
        layer_in[0],
        upstream[0],
    )
    return lg[None], hg[None], sg[None], wg, ig


def solution(mesh):
    placed = (
        P("dp", "ctx", None),
        P("dp", "ctx", "tensor"),
        P("dp", "ctx", "tensor"),
        P("tensor"),
        P("tensor"),
        P("tensor"),
        P("dp", "tensor", None),
        P("dp", "tensor"),
        P("dp", "ctx", None),
        P("dp"),
        P("dp"),
    )
    return jax.shard_map(
        per_device,
        mesh=mesh,
        in_specs=placed,
        out_specs=(
            P("dp", "ctx", None),
            P("dp", "ctx", "tensor"),
            P("dp", "ctx", "tensor"),
            P(("dp", "ctx"), "tensor"),
            P(("dp", "ctx"), "tensor", None),
        ),
        check_vma=False,
    )
```

```python
import jax
import jax.numpy as jnp
from jax import lax
from jax.experimental import pallas as pl
from jax.experimental.pallas import tpu as pltpu
from jax.sharding import PartitionSpec as P

f32 = jnp.float32
bf16 = jnp.bfloat16
MESH = pl.DeviceIdType.MESH
ANY = pl.BlockSpec(memory_space=pl.ANY)
VM = pl.BlockSpec(memory_space=pltpu.VMEM)
WINDOW = 3
LIMIT = 56 * 1024 * 1024
ROWS = (((0,), (0,)), ((), ()))
COLS = (((1,), (1,)), ((), ()))


def remote(src, dst, send, recv, where):
    return pltpu.make_async_remote_copy(
        src_ref=src, dst_ref=dst, send_sem=send, recv_sem=recv, device_id=where, device_id_type=MESH
    )


def greet(partners):
    barrier = pltpu.get_barrier_semaphore()
    for where in partners:
        pl.semaphore_signal(barrier, inc=1, device_id=where, device_id_type=MESH)
    pl.semaphore_wait(barrier, len(partners))


def places():
    x = lax.axis_index("dp")
    c = lax.axis_index("ctx")
    t = lax.axis_index("tensor")
    z = lax.rem(c, 8)
    base = c - z
    spots = dict(
        right={"dp": lax.rem(x + 1, 4)},
        left={"dp": lax.rem(x + 3, 4)},
        up={"ctx": base + lax.rem(z + 1, 8)},
        down={"ctx": base + lax.rem(z + 7, 8)},
        across={"ctx": lax.rem(c + 8, 16)},
        core={"tensor": t + 1 - 2 * lax.rem(t, 2)},
        far={"tensor": lax.rem(t + 2, 4)},
    )
    return x, c, t, z, spots


def dot(a, b, dims=None):
    if dims is None:
        return jnp.dot(a, b, preferred_element_type=f32)
    return lax.dot_general(a, b, dims, preferred_element_type=f32)


def pieces(v, count):
    found = []
    for _ in range(count):
        part = v.astype(bf16)
        found.append(part)
        v = v - part.astype(f32)
    return found


def split_left(v, m, count, dims=None):
    return sum(dot(part, m, dims) for part in pieces(v, count))


def split_right(m, v, count, dims=None):
    return sum(dot(m, part, dims) for part in pieces(v, count))


def iota(shape, axis):
    return lax.broadcasted_iota(jnp.int32, shape, axis)


class Lane:
    def __init__(self, window):
        self.window = window
        self.sent = []
        self.waited = 0

    def push(self, copy):
        while len(self.sent) - self.waited >= self.window:
            self.sent[self.waited].wait_send()
            self.waited += 1
        copy.start()
        self.sent.append(copy)

    def drain(self):
        while self.waited < len(self.sent):
            self.sent[self.waited].wait_send()
            self.waited += 1


def kernel(
    x_ref, raw_ref, bias_ref, rate_ref, skip_ref, start_ref, stop_ref, wi, wo, lin, up,
    lg, hg_ref, sg_ref, wg, ig,
    wi_v, wo_v, lin_v, up_v, proj_s, y_s, z_s, xs_s, xe_s, dy_s, de_s, erx_s, etx_s, dtx_s, ds_s,
    r_s, rt_s, grow_s, w_s, f_out, f_got, f_mid, f_fin, b_out, b_got, b_mid, b_fin,
    factor, act, part, half_out, half_in, pair_out, pair_in, acc, ring_out, ring_in, y_out, y_in, d_out, d_got,
    wsend, wrecv, asend, arecv, csend, crecv, esend, erecv,
    send, recv, zsend, zrecv, ysend, yrecv, tsend, trecv, local,
):
    x, c, t, z, at = places()
    h = lax.rem(z, 2)
    yl = lax.div(c, 8)
    cr = lax.rem(t, 2)
    lefts, rights, opposite = lax.rem(x + 3, 4), lax.rem(x + 1, 4), lax.rem(x + 2, 4)
    mine = pl.ds(pl.multiple_of(cr * 128, 128), 128)
    other = pl.ds(pl.multiple_of((1 - cr) * 128, 128), 128)

    def quarter(j):
        return pl.ds(pl.multiple_of(j * 512, 512), 512)

    loads = [
        pltpu.make_async_copy(wi, wi_v.at[quarter(x)], local.at[0]),
        pltpu.make_async_copy(wo, wo_v.at[quarter(x)], local.at[1]),
        pltpu.make_async_copy(lin, lin_v, local.at[2]),
        pltpu.make_async_copy(up, up_v, local.at[3]),
    ]
    for load in loads:
        load.start()
    greet(
        [at[k] for k in ("right", "left", "core", "far")]
        + [{"dp": opposite}]
        + [{"ctx": lax.rem(c + k, 16)} for k in range(1, 16)]
    )

    links = {k: Lane(WINDOW) for k in ("right", "left", "up", "down", "across")}
    halves = (h, yl, h)
    relays = (("up", "down"), ("across", "across"), ("up", "down"))

    def strip(ref, g):
        return ref if g == 0 else ref.at[:, 512 * (g - 1) : 512 * g]

    def weight_rows(g, slab, half, q):
        rows = pl.ds(pl.multiple_of(slab * 512 + half * 256 + q * 128, 128), 128)
        return strip(wi_v if g == 0 else wo_v, g).at[rows]

    def first(g, q, event, way):
        rows = pl.ds(pl.multiple_of(halves[g] * 256 + q * 128, 128), 128)
        links[way].push(
            remote(
                strip(wi if g == 0 else wo, g).at[rows],
                weight_rows(g, x, halves[g], q),
                wsend.at[g, event],
                wrecv.at[g, event],
                at[way],
            )
        )

    def arrived(g, slab, half, q, event):
        dst = weight_rows(g, slab, half, q)
        remote(dst, dst, wsend.at[g, event], wrecv.at[g, event], at["left"]).wait_recv()

    def forward(g, slab, q, event, way):
        dst = weight_rows(g, slab, halves[g], q)
        links[way].push(remote(dst, dst, wsend.at[g, event], wrecv.at[g, event], at[way]))

    def slot(g, n):
        h, (first_way, second_way) = halves[g], relays[g]
        if n == 0:
            first(g, 0, 0, "right")
            first(g, 1, 2, "left")
        elif n == 1:
            first(g, 1, 1, "right")
            first(g, 0, 3, "left")
        elif n == 2:
            arrived(g, lefts, h, 0, 0)
            forward(g, lefts, 0, 4, "right")
            arrived(g, rights, h, 1, 2)
            forward(g, rights, 1, 5, "left")
            forward(g, lefts, 0, 6, first_way)
            forward(g, rights, 1, 10, second_way)
        elif n == 3:
            arrived(g, lefts, h, 1, 1)
            forward(g, lefts, 1, 9, second_way)
            arrived(g, rights, h, 0, 3)
            forward(g, rights, 0, 7, first_way)
        else:
            arrived(g, opposite, h, 0, 4)
            forward(g, opposite, 0, 8, first_way)
            arrived(g, opposite, h, 1, 5)
            forward(g, opposite, 1, 11, second_way)

    def gathered(g):
        for n, slab in enumerate((lefts, rights, opposite)):
            arrived(g, slab, 1 - halves[g], 0, 6 + n)
            arrived(g, slab, 1 - halves[g], 1, 9 + n)

    def swap(e, src, dst):
        def to_peer(k):
            to = lax.rem(c + k, 16)
            return remote(src.at[to], dst.at[c], esend.at[e, k], erecv.at[e, k], {"ctx": to})

        def from_peer(k):
            who = lax.rem(c + 16 - k, 16)
            return remote(src.at[who], dst.at[who], esend.at[e, k], erecv.at[e, k], {"ctx": who})

        def each(fn):
            def step(k, carry):
                fn(k)
                return carry

            lax.fori_loop(1, 16, step, 0, unroll=True)

        def begin():
            each(lambda k: to_peer(k).start())
            dst[c] = src[c]

        return (
            begin,
            lambda: each(lambda k: from_peer(k).wait_recv()),
            lambda: each(lambda k: to_peer(k).wait_send()),
        )

    f1 = swap(0, f_out, f_got)
    f2 = swap(1, f_mid, f_fin)
    b1 = swap(2, b_out, b_got)
    b2 = swap(3, b_mid, b_fin)
    sums_out = {2: swap(4, d_out.at[0], d_got.at[0]), 3: swap(5, d_out.at[1], d_got.at[1])}

    slot(0, 0)
    slot(0, 1)

    side16 = iota((16, 1024), 1) - 64 * iota((16, 1024), 0)
    expand = jnp.where((side16 >= 0) & (side16 < 64), 1.0, 0.0).astype(bf16)
    above = iota((256, 256), 0) >= iota((256, 256), 1)
    tril = jnp.where(above, 1.0, 0.0).astype(bf16)
    eye = jnp.where(iota((256, 256), 0) == iota((256, 256), 1), 1.0, 0.0).astype(bf16)
    position = c * 256 + iota((256, 1), 0)
    mask = jnp.where((position >= start_ref[...]) & (position < stop_ref[...]), 1.0, 0.0)
    rate = jnp.exp(rate_ref[...])
    shifted = split_right(eye, raw_ref[...], 3, COLS) + bias_ref[...]
    small = jnp.exp(-jnp.abs(shifted))
    dt = mask * (jnp.maximum(shifted, 0.0) + jnp.log1p(small))
    sig = mask * jnp.where(shifted >= 0.0, 1.0, small) / (1.0 + small)
    running = split_right(tril, -dt * rate, 3)
    r_s[...] = running
    rt = split_left(running, eye, 3, ROWS)
    rt_s[...] = rt
    last = running[255:256, :]
    erx_s[...] = split_left(jnp.exp(running), expand, 2)
    etx_s[...] = split_left(jnp.exp(last - running), expand, 2)
    dtx_s[...] = split_left(dt, expand, 2)
    xs_s[...] = (x_ref[...].astype(f32) * dtx_s[...]).astype(bf16)
    xe_s[...] = (xs_s[...].astype(f32) * etx_s[...]).astype(bf16)
    skipx = split_left(jnp.broadcast_to(skip_ref[...], (8, 16)), expand, 3)[0:1, :]
    decay = jnp.broadcast_to(rt[:, 255:256], (16, 128))
    row = iota((16, 16, 128), 1)
    lines = jnp.zeros((16, 16, 128), f32)
    for n, term in enumerate(pieces(decay, 3)):
        lines = jnp.where(row == n, term.astype(f32)[:, None, :], lines)
    f_out[:, 64:80, :] = lines.astype(bf16)

    slot(0, 2)
    slot(1, 0)
    slot(0, 3)
    slot(1, 1)
    slot(0, 4)
    slot(1, 2)
    slot(2, 0)
    for load in loads:
        load.wait()
    gathered(0)

    def spans(g):
        return slice(512 * g, 512 * g + 512)

    def bs(g):
        return proj_s[:, 256 * g : 256 * g + 128]

    def cs(g):
        return proj_s[:, 256 * g + 128 : 256 * g + 256]

    proj_s[...] = dot(lin_v[...], wi_v[...]).astype(bf16)
    for g in range(2):
        own = dot(xe_s[:, spans(g)], bs(g), ROWS)
        f_out[8 * g : 8 * g + 8, 0:64, :] = own.reshape(8, 64, 128).astype(bf16)
    f1[0]()
    slot(1, 3)
    slot(2, 1)
    slot(1, 4)
    slot(2, 2)
    slot(2, 3)

    def grow_of(k):
        lines = f_got[k, 64:80, :].astype(f32)
        return jnp.exp(lines[0:1] + lines[1:2] + lines[2:3])

    f1[1]()

    def ahead(k, state):
        f_mid[k] = state.astype(bf16)
        return grow_of(k) * state + f_got[k, 0:64, :].astype(f32)

    lax.fori_loop(0, 16, ahead, jnp.zeros((64, 128), f32), unroll=True)
    f2[0]()
    slot(2, 4)

    values = (up_v, lin_v)
    acts = []

    def token_rows(r):
        return pl.ds(pl.multiple_of(r * 64, 64), 64)

    far_t, core_t = lax.rem(t + 2, 4), t + 1 - 2 * cr
    fourth_t = lax.rem(core_t + 2, 4)

    def act_send(n):
        for k in (1, 3, 2):
            to = lax.rem(x + k, 4)
            copy = remote(
                values[n].at[token_rows(t), quarter(to)],
                act.at[n, x, token_rows(t)],
                asend.at[n, k],
                arecv.at[n, k],
                {"dp": to},
            )
            copy.start()
            acts.append(copy)
        act[n, x] = values[n][:, quarter(x)]

    def act_move(n, k, r, event, way):
        dst = act.at[n, lax.rem(x + 4 - k, 4), token_rows(r)]
        return remote(dst, dst, csend.at[n, k, event], crecv.at[n, k, event], at[way])

    def act_share(n):
        for k in (1, 3, 2):
            dst = act.at[n, lax.rem(x + 4 - k, 4), token_rows(t)]
            remote(dst, dst, asend.at[n, k], arecv.at[n, k], at["left"]).wait_recv()
            for event, way in ((0, "far"), (1, "core")):
                copy = act_move(n, k, t, event, way)
                copy.start()
                acts.append(copy)

    def act_pass(n):
        for k in (1, 3, 2):
            act_move(n, k, far_t, 0, "far").wait_recv()
            copy = act_move(n, k, far_t, 2, "core")
            copy.start()
            acts.append(copy)

    def act_done(n):
        for k in (1, 3, 2):
            act_move(n, k, core_t, 1, "core").wait_recv()
            act_move(n, k, fourth_t, 2, "core").wait_recv()

    side = iota((256, 128), 1)
    side16 = iota((256, 16), 1)
    low_side = side < 64

    def half_of(v, half):
        return jnp.where(low_side if half == 0 else ~low_side, v, jnp.zeros_like(v))

    def lanes_of(g, p):
        return pl.ds(pl.multiple_of(512 * g + p * 128, 128), 128)

    def ahead_group(g):
        scores = dot(cs(g), bs(g), COLS)

        def pair(p, carry):
            x2 = xs_s[:, lanes_of(g, p)]
            y2 = jnp.zeros((256, 128), f32)
            for half in range(2):
                head = 8 * g + 2 * p + half
                col = jnp.sum(jnp.where(side16 == head, r_s[...], 0.0), axis=1, keepdims=True)
                line = rt_s[pl.ds(head, 1), :]
                grow = jnp.exp(jnp.where(above, col - line, -1e30))
                w = (scores * grow).astype(bf16)
                grow_s[head] = grow
                w_s[head] = w
                y2 += dot(w, half_of(x2, half))
            y_s[:, lanes_of(g, p)] = y2
            return carry

        lax.fori_loop(0, 4, pair, 0)

    def back_group(g):
        ds_s[g] = jnp.zeros((256, 256), f32)

        def pair(p, carry):
            x2 = xs_s[:, lanes_of(g, p)]
            dy2 = dy_s[:, lanes_of(g, p)]
            z2 = jnp.zeros((256, 128), f32)
            ds = ds_s[g]
            for half in range(2):
                head = 8 * g + 2 * p + half
                dm = half_of(dy2, half)
                z2 += dot(w_s[head], dm, ROWS)
                ds += dot(dm, half_of(x2, half), COLS) * grow_s[head]
            z_s[:, lanes_of(g, p)] = z2
            ds_s[g] = ds
            return carry

        lax.fori_loop(0, 4, pair, 0)

    act_send(0)
    act_send(1)
    ahead_group(0)
    ahead_group(1)
    gathered(1)
    dy_s[:, 0:512] = (dot(up_v[...], wo_v[:, 0:512]).astype(bf16).astype(f32) * mask).astype(bf16)
    def states(fin, g):
        return fin[8 * g : 8 * g + 8].reshape(512, 128)

    sent = []

    def go(copy):
        copy.start()
        sent.append(copy)

    def view(ref, g, *index):
        if g < 2:
            return ref.at[(g,) + index]
        tail = (slice(None),) * (len(ref.shape) - 2 - len(index))
        return ref.at[(2,) + index + tail + (slice(256 * g - 512, 256 * g - 256),)]

    def rows_of(g, slab, q):
        rows = pl.ds(128 * q, 128)
        if g < 2:
            return factor.at[g, slab, rows]
        return factor.at[2, slab, rows, 256 * g - 512 : 256 * g - 256]

    def own_send(g):
        for q, event, way in ((0, 0, "right"), (1, 2, "left"), (1, 1, "right"), (0, 3, "left")):
            src = rows_of(g, x, q)
            go(remote(src, src, send.at[g, event], recv.at[g, event], at[way]))

    def came(g, slab, q, event):
        dst = rows_of(g, slab, q)
        remote(dst, dst, send.at[g, event], recv.at[g, event], at["left"]).wait_recv()
        return dst

    def relay(g):
        src = came(g, lefts, 0, 0)
        go(remote(src, src, send.at[g, 4], recv.at[g, 4], at["right"]))
        src = came(g, rights, 1, 2)
        go(remote(src, src, send.at[g, 5], recv.at[g, 5], at["left"]))

    f2[1]()
    for g in range(2):
        span = spans(g)
        ya = dot(cs(g), states(f_fin, g), COLS) * erx_s[:, span]
        yt = y_s[:, span] + ya
        y_s[:, span] = yt
        value = mask * (yt + skipx[:, span] * x_ref[:, span].astype(f32))
        factor[g, x] = value.astype(bf16)
        own_send(g)
    gathered(2)
    dy_s[:, 512:] = (dot(up_v[...], wo_v[:, 512:]).astype(bf16).astype(f32) * mask).astype(bf16)
    de_s[...] = (dy_s[...].astype(f32) * erx_s[...]).astype(bf16)
    for g in range(2):
        pull = dot(de_s[:, spans(g)], cs(g), ROWS)
        b_out[8 * g : 8 * g + 8] = pull.reshape(8, 64, 128).astype(bf16)
    b1[0]()

    act_share(0)
    act_share(1)
    back_group(0)
    back_group(1)

    b1[1]()

    def behind(n, state):
        k = 15 - n
        b_mid[k] = state.astype(bf16)
        return grow_of(k) * state + b_got[k].astype(f32)

    lax.fori_loop(0, 16, behind, jnp.zeros((64, 128), f32), unroll=True)
    b2[0]()
    act_pass(0)
    act_pass(1)
    relay(0)
    relay(1)
    b2[1]()

    for g in range(2):
        later = states(b_fin, g)
        state = states(f_fin, g)
        dsr = ds_s[g].astype(bf16)
        db = dot(dsr, cs(g), ROWS) + dot(xe_s[:, spans(g)], later)
        dc = dot(dsr, bs(g)) + dot(de_s[:, spans(g)], state)
        factor[2, x, :, 256 * g : 256 * g + 128] = db.astype(bf16)
        factor[2, x, :, 256 * g + 128 : 256 * g + 256] = dc.astype(bf16)
        own_send(2 + g)
    part[...] = dot(factor[2, x], wi_v[...], COLS)
    half_out[...] = part[other, :].astype(bf16)
    go(remote(half_out, half_in, tsend.at[0], trecv.at[0], at["core"]))

    def product(g):
        came(g, lefts, 1, 1)
        came(g, rights, 0, 3)
        came(g, opposite, 0, 4)
        came(g, opposite, 1, 5)
        a = act[0 if g < 2 else 1].reshape(1024, 512)
        if g < 2:
            acc[g] = dot(a, factor[g].reshape(1024, 512), ROWS).reshape(16, 32, 512)
        else:
            lanes = slice(256 * g - 512, 256 * g - 256)
            right = factor[2, :, :, lanes].reshape(1024, 256)
            acc[2, :, :, lanes] = dot(a, right, ROWS).reshape(16, 32, 256)

    def arrival(g, n):
        got = view(ring_in, g, n)
        remote(got, got, zsend.at[g, n], zrecv.at[g, n], at["up"]).wait_recv()
        return got[0].astype(f32), got[1].astype(f32)

    def pass_on(g, k, slot_in, slot_out, way):
        low, high = view(acc, g, k)[...], view(acc, g, 8 + k)[...]
        if slot_in is not None:
            more = arrival(g, slot_in)
            low += more[0]
            high += more[1]
        src, dst = view(ring_out, g, slot_out), view(ring_in, g, slot_out)
        src[0] = low.astype(bf16)
        src[1] = high.astype(bf16)
        go(remote(src, dst, zsend.at[g, slot_out], zrecv.at[g, slot_out], at[way]))

    def ring(g, s):
        if s < 4:
            pass_on(g, lax.rem(z + 4 - s, 8), s - 1 if s else None, s, "up")
        if s < 3:
            pass_on(g, lax.rem(z + 5 + s, 8), s + 3 if s else None, s + 4, "down")
        if s == 4:
            low, high = view(acc, g, z)[...], view(acc, g, 8 + z)[...]
            for n in (3, 6):
                more = arrival(g, n)
                low += more[0]
                high += more[1]
            view(acc, g, z)[...] = low
            view(acc, g, 8 + z)[...] = high
            src, dst = view(y_out, g), view(y_in, g)
            src[...] = view(acc, g, (1 - yl) * 8 + z)[...].astype(bf16)
            go(remote(src, dst, ysend.at[g], yrecv.at[g], at["across"]))

    def finish(g):
        src, dst = view(y_out, g), view(y_in, g)
        remote(src, dst, ysend.at[g], yrecv.at[g], at["across"]).wait_recv()
        total = view(acc, g, c)[...] + dst[...].astype(f32)
        if g < 2:
            wg[:, 512 * g : 512 * g + 512] = total
        else:
            ig[:, 256 * g - 512 : 256 * g - 256] = total

    sums_q = jnp.zeros((256, 16), f32)
    sums_v = jnp.zeros((256, 16), f32)
    sums_u = jnp.zeros((256, 16), f32)
    ends = jnp.zeros((8, 16), f32)
    sums = (sums_q, sums_v, sums_u, ends)
    ones = jnp.ones((8, 128), bf16)
    def rest(g, sums):
        sums_q, sums_v, sums_u, ends = sums
        span = spans(g)
        later, state = states(b_fin, g), states(f_fin, g)
        ex = expand[:, span]
        zs = dot(bs(g), later, COLS) * etx_s[:, span]
        xg = x_ref[:, span].astype(f32)
        xsg = xs_s[:, span].astype(f32)
        dyg = dy_s[:, span].astype(f32)
        zw = z_s[:, span]
        zt = zw + zs
        hg_ref[:, span] = (dtx_s[:, span] * zt + skipx[:, span] * dyg).astype(bf16)
        sums_q += split_left(dyg * y_s[:, span] - xsg * zw, ex, 3, COLS)
        sums_v += split_left(xsg * zs, ex, 2, COLS)
        sums_u += split_left(xg * zt, ex, 2, COLS)
        rows = split_right(ones, state.astype(f32) * later.astype(f32), 2, COLS)
        ends += split_left(rows, ex, 2, COLS)
        return sums_q, sums_v, sums_u, ends

    act_done(0)
    product(0)
    ring(0, 0)
    relay(2)
    product(1)
    ring(1, 0)
    ring(0, 1)
    relay(3)
    ring(1, 1)
    remote(half_out, half_in, tsend.at[0], trecv.at[0], at["core"]).wait_recv()
    pair_out[...] = (part[mine, :] + half_in[...].astype(f32)).astype(bf16)
    go(remote(pair_out, pair_in, tsend.at[1], trecv.at[1], at["far"]))
    act_done(1)
    product(2)
    d_out[0] = view(acc, 2)[...].astype(bf16)
    sums_out[2][0]()
    ring(0, 2)
    ring(1, 2)
    sums = rest(0, sums)
    product(3)
    d_out[1] = view(acc, 3)[...].astype(bf16)
    sums_out[3][0]()
    ring(0, 3)
    ring(1, 3)
    sums = rest(1, sums)
    ring(0, 4)
    ring(1, 4)
    remote(pair_out, pair_in, tsend.at[1], trecv.at[1], at["far"]).wait_recv()
    lg[mine, :] = (pair_out[...].astype(f32) + pair_in[...].astype(f32)).astype(bf16)
    go(remote(lg.at[mine], lg.at[mine], tsend.at[2], trecv.at[2], at["core"]))
    sums_q, sums_v, sums_u, ends = sums
    triu = jnp.where(iota((256, 256), 0) <= iota((256, 256), 1), 1.0, 0.0).astype(bf16)
    lower = jnp.where(iota((256, 256), 0) > iota((256, 256), 1), 1.0, 0.0).astype(bf16)
    flow = split_right(triu, sums_q, 3) + split_right(lower, sums_v, 3)
    flow = flow + ends[0:1, :] * jnp.exp(last)
    sg_ref[...] = sig * (sums_u - rate * flow)

    finish(0)
    finish(1)
    for lane in links.values():
        lane.drain()
    for copy in acts:
        copy.wait_send()
    for e in (f1, f2, b1, b2):
        e[2]()
    sums_out[2][1]()
    sums_out[2][2]()
    ig[:, 0:256] = jnp.sum(d_got[0].astype(f32), axis=0)
    sums_out[3][1]()
    sums_out[3][2]()
    ig[:, 256:512] = jnp.sum(d_got[1].astype(f32), axis=0)
    remote(lg.at[other], lg.at[other], tsend.at[2], trecv.at[2], at["core"]).wait_recv()
    for copy in sent:
        copy.wait_send()


def whole(x, raw, bias, rate, skip, start, stop, wi, wo, lin, up):
    def vm(shape, kind=bf16):
        return pltpu.VMEM(shape, kind)

    dma = pltpu.SemaphoreType.DMA
    return pl.pallas_call(
        kernel,
        out_shape=(
            jax.ShapeDtypeStruct((256, 2048), bf16),
            jax.ShapeDtypeStruct((256, 1024), bf16),
            jax.ShapeDtypeStruct((256, 16), f32),
            jax.ShapeDtypeStruct((32, 1024), f32),
            jax.ShapeDtypeStruct((32, 512), f32),
        ),
        in_specs=[VM] * 7 + [ANY] * 4,
        out_specs=(VM,) * 5,
        scratch_shapes=[
            vm((2048, 512)), vm((2048, 1024)), vm((256, 2048)), vm((256, 2048)),
            vm((256, 512)), vm((256, 1024), f32), vm((256, 1024), f32),
            vm((256, 1024)), vm((256, 1024)), vm((256, 1024)), vm((256, 1024)),
            vm((256, 1024), f32), vm((256, 1024), f32), vm((256, 1024), f32),
            vm((2, 256, 256), f32), vm((256, 16), f32), vm((16, 256), f32), vm((16, 256, 256), f32), vm((16, 256, 256)),
            vm((16, 80, 128)), vm((16, 80, 128)), vm((16, 64, 128)), vm((16, 64, 128)),
            vm((16, 64, 128)), vm((16, 64, 128)), vm((16, 64, 128)), vm((16, 64, 128)),
            vm((3, 4, 256, 512)), vm((2, 4, 256, 512)),
            vm((256, 2048), f32), vm((128, 2048)), vm((128, 2048)), vm((128, 2048)), vm((128, 2048)),
            vm((3, 16, 32, 512), f32), vm((3, 7, 2, 32, 512)), vm((3, 7, 2, 32, 512)),
            vm((3, 32, 512)), vm((3, 32, 512)), vm((2, 16, 32, 256)), vm((2, 16, 32, 256)),
            dma((3, 12)), dma((3, 12)), dma((2, 4)), dma((2, 4)), dma((2, 4, 3)), dma((2, 4, 3)),
            dma((6, 16)), dma((6, 16)),
            dma((4, 6)), dma((4, 6)), dma((4, 7)), dma((4, 7)), dma((4,)), dma((4,)), dma((3,)), dma((3,)),
            dma((4,)),
        ],
        compiler_params=pltpu.CompilerParams(
            collective_id=1, has_side_effects=True, vmem_limit_bytes=LIMIT
        ),
        name="whole",
    )(x, raw, bias, rate, skip, start, stop, wi, wo, lin, up)


def settle_kernel(lg, hg, sg, wg, ig, lg_out, hg_out, sg_out, wg_out, ig_out):
    lg_out[...] = lg[...]
    hg_out[...] = hg[...]
    sg_out[...] = sg[...]
    wg_out[...] = wg[...]
    ig_out[:, 0, :] = ig[:, 0:256]
    ig_out[:, 1, :] = ig[:, 256:512]


def settle(*found):
    shapes = [(v.shape, v.dtype) for v in found[:4]] + [((32, 2, 256), f32)]

    def rows(shape):
        rest = tuple(shape[1:])
        return pl.BlockSpec((shape[0] // 4,) + rest, lambda n: (n,) + (0,) * len(rest))

    return pl.pallas_call(
        settle_kernel,
        out_shape=tuple(jax.ShapeDtypeStruct(*kind) for kind in shapes),
        grid=(4,),
        in_specs=[rows(v.shape) for v in found],
        out_specs=tuple(rows(shape) for shape, _ in shapes),
        name="settle",
    )(*found)


def call(*inputs):
    return settle(*whole(*inputs))


def per_device(
    layer_in, head_in, step_raw, step_bias, rate_log, skip_gain,
    inject_weight, out_weight, upstream, window_start, lengths,
):
    lg, hg, sg, wg, ig = call(
        head_in[0],
        step_raw[0].T,
        step_bias[None],
        rate_log[None],
        skip_gain[None],
        window_start[None],
        lengths[None],
        inject_weight.reshape(512, 512),
        out_weight,
        layer_in[0],
        upstream[0],
    )
    return lg[None], hg[None], sg[None], wg, ig


def solution(mesh):
    placed = (
        P("dp", "ctx", None),
        P("dp", "ctx", "tensor"),
        P("dp", "ctx", "tensor"),
        P("tensor"),
        P("tensor"),
        P("tensor"),
        P("dp", "tensor", None),
        P("dp", "tensor"),
        P("dp", "ctx", None),
        P("dp"),
        P("dp"),
    )
    return jax.shard_map(
        per_device,
        mesh=mesh,
        in_specs=placed,
        out_specs=(
            P("dp", "ctx", None),
            P("dp", "ctx", "tensor"),
            P("dp", "ctx", "tensor"),
            P(("dp", "ctx"), "tensor"),
            P(("dp", "ctx"), "tensor", None),
        ),
        check_vma=False,
    )
```
